32 devices in a mesh: gx: 2 (over x), az: 4 (over y, core), ta: 4 (over z).
Axes of the slice: x: 2, y: 2, z: 4, core: 2. Of those that a mesh axis runs over, the one named last changes fastest.
Arguments:
- velocity: float32 [32, 32, 1024], P('gx', 'az', 'ta'), may hold values from -6 to 6
- pressure: float32 [32, 32, 1024], P('gx', 'az', 'ta'), may hold values from -6 to 6
- offsets: int32 [8], replicated, may hold values from 1 to 16, as said below
Outputs:
- correlation: float32 [32, 8, 1056], P(('gx', 'az', 'ta'))
The draws below stay inside these ranges and needn't reach their ends.
Inputs may be any that keep to these rules, and one draw needn't show every extreme that they name: `offsets`: the 8 separations are distinct and the largest equals 16.
All inputs are finite; a program needn't handle non-finite values.
Results may differ from the reference program's by a relative error of at most 0.00007.
Values sent between devices are 32-bit elements; how exact they have to be, the bound alone decides.
No kernel may reach another device: no remote copies, remote signals or barrier semaphores. Data moves between devices by JAX's collectives and lax.ppermute only.
A program may use at most 64 MiB of HBM per device.

```python
import math
import jax
import jax.numpy as jnp
from jax import lax

AZIM = 32
NBR = 8
SPAN = 16
MAXLAG = 16
LAGS = 33
STATIONS = 32
TIMES = 1024


def draw_offsets(key, part):
    shuffled = jax.random.permutation(key, SPAN - 1).astype(jnp.int32) + 1
    largest = jnp.full((1,), SPAN, jnp.int32)
    return jnp.concatenate([shuffled[:NBR - 1], largest]).astype(jnp.int32)


def steps_of(own_key, dims, shards, least, high):
    factor_of, own = 1.0, jax.random.fold_in(own_key, 6)
    for position, blocks in shards:
        steps = jnp.exp(jax.random.uniform(jax.random.fold_in(own, position), (blocks,), jnp.float32, least / len(shards), high / len(shards)))
        factor_of = factor_of * jnp.repeat(steps, dims[position] // blocks).reshape([-1 if axis == position else 1 for axis in range(len(dims))])
    return factor_of


def scatter_about(rng, shape, width, most, shards=(), kind=jnp.bfloat16):
    entries = jax.random.normal(rng, shape, jnp.float32) * width
    if len(shards) > 0:
        entries = steps_of(rng, shape, shards, -0.22, 0.18) * entries
    return jnp.clip(entries, min=-most, max=most).astype(kind)


def setup_inputs(seed: int = 0) -> dict:
    arg_keys = jax.random.split(jax.random.key(seed), 4)
    return {
        "velocity": scatter_about(arg_keys[0], (STATIONS, AZIM, TIMES), 1.0, 6.0, ((0, 2), (1, 4), (2, 4)), jnp.float32),
        "pressure": scatter_about(arg_keys[1], (STATIONS, AZIM, TIMES), 1.0, 6.0, ((0, 2), (1, 4), (2, 4)), jnp.float32),
        "offsets": draw_offsets(jax.random.fold_in(arg_keys[3], 71), 0),
    }


def reference(velocity, pressure, offsets):
    length = 2 * TIMES
    factor = 1.0 / math.sqrt(TIMES * AZIM)
    vel_hat = jnp.fft.rfft2(velocity, s=(AZIM, length), axes=(1, 2))
    pres_ext = jnp.concatenate([pressure, jnp.zeros((SPAN, AZIM, TIMES), pressure.dtype)], axis=0)
    pres_hat = jnp.fft.rfft2(pres_ext, s=(AZIM, length), axes=(1, 2))

    def one_station(station):
        own_hat = jnp.conj(lax.dynamic_index_in_dim(vel_hat, station, 0, keepdims=False))
        partners = jnp.take(pres_hat, station + offsets, axis=0)
        inverse = jnp.fft.irfft2(own_hat[None] * partners, s=(AZIM, length), axes=(1, 2))
        window = jnp.concatenate([inverse[:, :, length - MAXLAG:], inverse[:, :, :MAXLAG + 1]], axis=2)
        return jnp.transpose(window, (0, 2, 1)).reshape(NBR, LAGS * AZIM) * factor
    result = lax.map(one_station, jnp.arange(STATIONS, dtype=jnp.int32))
    return result.astype(jnp.float32)
```

```python
import functools
import math

import jax
import jax.numpy as jnp
from jax import lax
from jax.experimental import pallas as pl
from jax.experimental.pallas import tpu as pltpu
from jax.sharding import PartitionSpec as P

MAXLAG = 16
LAGS = 2 * MAXLAG + 1
MAIN = 2 * MAXLAG
LANES = 128
BF16 = jnp.bfloat16
F32 = jnp.float32


def split(x):
    high = x.astype(BF16)
    return high, (x - high.astype(F32)).astype(BF16)


def in_core_order(core, mine, other):
    first = jnp.where(core == 0, mine, other)
    second = jnp.where(core == 0, other, mine)
    return jnp.concatenate([first, second], axis=0)


def lag_kernel(info, v_own, v_sib, v_far, v_far_sib, h_own, h_sib, h_far, h_far_sib, out):
    step = pl.program_id(0)
    core, row_y = info[0], info[1]
    own, far = info[3] + step, info[4] + step
    rows, times = v_own.shape[1:]
    width = times + LANES
    far_v = far + v_far.shape[0] - h_far.shape[0]
    near = (v_own, v_sib, h_own, h_sib, own, own, row_y)
    away = (v_far, v_far_sib, h_far, h_far_sib, far_v, far, 1 - row_y)
    for v_a, v_b, h_a, h_b, at_v, at_h, place in (near, away):
        mine = jnp.concatenate([v_a[at_v], h_a[at_h]], axis=1)
        other = jnp.concatenate([v_b[at_v], h_b[at_h]], axis=1)
        series = in_core_order(core, mine, other)
        for b in range(2 * rows):
            line = jnp.broadcast_to(series[b : b + 1, :], (8, width))
            for half in range(MAIN // 16):
                parts = [
                    pltpu.roll(line, (8 * g - MAXLAG) % width, 1, stride=1, stride_axis=0)[:, :times]
                    for g in (2 * half, 2 * half + 1)
                ]
                high, low = split(jnp.concatenate(parts, axis=0))
                at = b * MAIN + 16 * half
                out[0, 0, place, at : at + 16, :] = high
                out[0, 1, place, at : at + 16, :] = low
        last = pltpu.roll(series, MAXLAG, 1)[:, :times]
        high, low = split(last)
        at = 2 * rows * MAIN
        out[0, 0, place, at : at + 2 * rows, :] = high
        out[0, 1, place, at : at + 2 * rows, :] = low


def turn(x, by, azim):
    lane = lax.broadcasted_iota(jnp.int32, x.shape, 1) % azim
    left = pltpu.roll(x, LANES - by, 1)
    right = pltpu.roll(x, azim - by, 1)
    return jnp.where(lane < azim - by, left, right)


def product_kernel(info, offsets, lags, o_own, u_own, near, upper, third,
                   o_sib, u_sib, near_sib, upper_sib, third_sib, *rest):
    outs, (high_p, low_p, prod) = rest[:-3], rest[-3:]
    step = pl.program_id(0)
    core, row_y, place, last_gx = info[0], info[1], info[2], info[5]
    half = third.shape[0]
    rows, times = o_own.shape[1:]
    azim = 4 * rows
    count = offsets.shape[0]

    @pl.when(step == 0)
    def _():
        keep_up = jnp.where(last_gx == 1, 0.0, 1.0).astype(F32)
        keep_mid = jnp.where((last_gx == 1) & (row_y == 1), 0.0, 1.0).astype(F32)

        def one(w, carry):
            def block(mine, other, keep=None):
                x = in_core_order(core, mine, other)
                return x if keep is None else x * keep

            def pick(a, b):
                return jnp.where(row_y == 0, a, b)

            shift = row_y * half
            found = {
                (0, 0): block(o_own[shift + w], o_sib[shift + w]),
                (0, 1): block(pick(o_own[half + w], u_own[w]), pick(o_sib[half + w], u_sib[w]), keep_mid),
                (0, 2): block(u_own[shift + w], u_sib[shift + w], keep_up),
                (1, 0): block(pick(third[w], near[w]), pick(third_sib[w], near_sib[w])),
                (1, 1): block(pick(near[w], upper[w]), pick(near_sib[w], upper_sib[w]), keep_mid),
                (1, 2): block(pick(upper[w], third[w]), pick(upper_sib[w], third_sib[w]), keep_up),
            }
            for (away, slot), x in found.items():
                high, low = split(x)
                at = jnp.where(row_y == away, 0, 1)
                high_p[slot * half + w, at] = high
                low_p[slot * half + w, at] = low
            return carry

        lax.fori_loop(0, half, one, 0)

    station = place ^ step
    first = (half // 2) * core + station
    right = []
    for turned in (0, 1):
        tiles = {0: [], 1: []}
        for k in range(count):
            w = first + offsets[k]
            for which, source in ((0, high_p), (1, low_p)):
                tiles[which] += [source[w, turned], source[w, 1 - turned]]
        high = jnp.concatenate(tiles[0], axis=0)
        low = jnp.concatenate(tiles[1], axis=0)
        right += [high, low, high]
    right = jnp.concatenate(right, axis=1)
    left = []
    for y in (0, 1):
        left += [lags[0, 0, y], lags[0, 0, y], lags[0, 1, y]]
    left = jnp.concatenate(left, axis=1)
    prod[...] = lax.dot_general(left, right, (((1,), (1,)), ((), ())), preferred_element_type=F32)

    pieces = []
    for c in range(0, count * azim, LANES):
        level = [prod[b * MAIN : (b + 1) * MAIN, c : c + LANES] for b in range(2 * rows)]
        by = 1
        while len(level) > 1:
            level = [level[i] + turn(level[i + 1], by, azim) for i in range(0, len(level), 2)]
            by *= 2
        extra = prod[2 * rows * MAIN : 2 * rows * (MAIN + 1), c : c + LANES]
        row = lax.broadcasted_iota(jnp.int32, extra.shape, 0)
        by = 1
        while by < 2 * rows:
            extra = jnp.where((row & by) != 0, turn(extra, by, azim), extra)
            by *= 2
        tail = jnp.broadcast_to(jnp.sum(extra, axis=0, keepdims=True), (8, LANES))
        pieces.append(jnp.concatenate([level[0], tail], axis=0))
    result = jnp.concatenate(pieces, axis=1)
    for i, out in enumerate(outs):
        @pl.when(step == i)
        def _(out=out):
            out[...] = result


def close_kernel(factor, count, azim, *refs):
    out = refs[-1]
    total = refs[0][...]
    for ref in refs[1:-1]:
        total = total + ref[...]
    total = total * factor
    groups = LANES // azim
    lane = lax.broadcasted_iota(jnp.int32, (count, LANES), 1) // azim
    sub = lax.broadcasted_iota(jnp.int32, (count, LANES), 0)
    for tile in range(-(-LAGS // groups)):
        acc = jnp.zeros((count, LANES), F32)
        for j in range(groups):
            tau = tile * groups + j
            if tau >= LAGS:
                continue
            x = jnp.zeros((count, LANES), F32)
            for part in range(count // groups):
                line = total[tau : tau + 1, part * LANES : (part + 1) * LANES]
                x = jnp.where(sub // groups == part, jnp.broadcast_to(line, (count, LANES)), x)
            moved = x
            for s in range(groups):
                by = ((j - s) * azim) % LANES
                shifted = pltpu.roll(x, by, 1) if by else x
                moved = jnp.where(sub % groups == s, shifted, moved)
            acc = jnp.where(lane == j, moved, acc)
        width = min(LANES, (LAGS - tile * groups) * azim)
        out[0, :, tile * LANES : tile * LANES + width] = acc[:, :width]


def whole(shape):
    return pl.BlockSpec(shape, lambda *_: (0,) * len(shape))


def lag_rows(info, *arrays):
    own = arrays[0]
    stations = info_stations(own)
    rows, times = own.shape[1:]
    height = 2 * rows * (MAIN + 1)
    shape = (stations, 2, 2, height, times)
    return pl.pallas_call(
        lag_kernel,
        grid_spec=pltpu.PrefetchScalarGridSpec(
            num_scalar_prefetch=1,
            grid=(stations,),
            in_specs=[whole(x.shape) for x in arrays],
            out_specs=pl.BlockSpec((1,) + shape[1:], lambda i, info: (i, 0, 0, 0, 0)),
        ),
        out_shape=jax.ShapeDtypeStruct(shape, BF16),
        compiler_params=pltpu.CompilerParams(vmem_limit_bytes=24 << 20),
        cost_estimate=pl.CostEstimate(flops=20_000_000, bytes_accessed=6 << 20, transcendentals=0),
    )(info, *arrays)


def info_stations(own):
    return own.shape[0] // 4


def products(info, offsets, lags, pieces):
    stations = lags.shape[0]
    half = pieces[4].shape[0]
    rows, times = pieces[0].shape[1:]
    columns = offsets.shape[0] * 4 * rows
    out = jax.ShapeDtypeStruct((MAIN + 8, columns), F32)
    window = (3 * half, 2, 2 * rows, times)
    return pl.pallas_call(
        product_kernel,
        grid_spec=pltpu.PrefetchScalarGridSpec(
            num_scalar_prefetch=2,
            grid=(stations,),
            in_specs=[
                pl.BlockSpec((1,) + lags.shape[1:], lambda i, info, off: (info[2] ^ i, 0, 0, 0, 0))
            ]
            + [whole(x.shape) for x in pieces],
            out_specs=[whole(out.shape)] * stations,
            scratch_shapes=[
                pltpu.VMEM(window, BF16),
                pltpu.VMEM(window, BF16),
                pltpu.VMEM((lags.shape[3], columns), F32),
            ],
        ),
        out_shape=[out] * stations,
        compiler_params=pltpu.CompilerParams(vmem_limit_bytes=32 << 20),
        cost_estimate=pl.CostEstimate(
            flops=2 * 3 * stations * 2 * lags.shape[3] * times * columns,
            bytes_accessed=8 << 20, transcendentals=0,
        ),
    )(info, offsets, lags, *pieces)


def close(parts, factor, count, azim):
    return pl.pallas_call(
        functools.partial(close_kernel, factor, count, azim),
        out_shape=jax.ShapeDtypeStruct((1, count, LAGS * azim), F32),
        cost_estimate=pl.CostEstimate(flops=1_000_000, bytes_accessed=1 << 18, transcendentals=0),
    )(*parts)


def shards(velocity, pressure, offsets):
    sta, rows, times = velocity.shape
    gx_n, az_n, ta_n = (lax.axis_size(name) for name in ("gx", "az", "ta"))
    gx, az, ta = (lax.axis_index(name) for name in ("gx", "az", "ta"))
    assert az_n == 4 and sta == az_n * ta_n
    half, mine = sta // 2, sta // az_n
    core, row_y = az % 2, az // 2
    azim = rows * az_n
    factor = 1.0 / math.sqrt(times * ta_n * azim)

    sibling = [(i, i ^ 1) for i in range(az_n)]
    across = [(i, i ^ 2) for i in range(az_n)]
    gx_az = [(g, a) for g in range(gx_n) for a in range(az_n)]
    flat = lambda g, a: (g % gx_n) * az_n + a
    upstream = [(g, (g - 1) % gx_n) for g in range(gx_n)]
    diagonal = [(flat(g, a), flat(g - 1, a ^ 2)) for g, a in gx_az]
    mixed = [(flat(g, a), flat(g, a ^ 2) if a >= 2 else flat(g - 1, a ^ 2)) for g, a in gx_az]
    pair = lambda i: i if not 0 <= i < ta_n else i
    even_odd = [(i, i ^ 1 if (i ^ 1) < ta_n else i) for i in range(ta_n)]
    odd_even = [(i, min(max(((i + 1) ^ 1) - 1, 0), ta_n - 1)) for i in range(ta_n)]

    to_sibling = lambda x: lax.ppermute(x, "az", sibling)

    info = jnp.stack([
        core, row_y, ta, mine * az, mine * core, (gx == gx_n - 1).astype(jnp.int32),
    ]).astype(jnp.int32)

    left_edge, right_edge = velocity[:, :, :LANES], velocity[:, :, times - LANES :]
    even = ta % 2 == 0
    got_a = lax.ppermute(jnp.where(even, right_edge, left_edge), "ta", even_odd)
    got_b = lax.ppermute(jnp.where(even, left_edge, right_edge), "ta", odd_even)

    v_for = lax.dynamic_slice_in_dim(velocity, half * (1 - row_y), half, 0)
    far = lax.ppermute(jnp.concatenate([pressure[half:], v_for], axis=0), "az", across)
    up = lax.ppermute(pressure, "gx", upstream)
    upper = lax.ppermute(pressure[:half], ("gx", "az"), diagonal)
    third = lax.ppermute(jnp.where(row_y == 1, pressure[:half], pressure[half:]), ("gx", "az"), mixed)

    before = jnp.where(even, got_b, got_a) * (ta > 0).astype(F32)
    after = jnp.where(even, got_a, got_b) * (ta < ta_n - 1).astype(F32)
    lane = lax.broadcasted_iota(jnp.int32, before.shape, 2)
    halo = jnp.where(lane < LANES // 2, after, before)
    halo_for = lax.dynamic_slice_in_dim(halo, half * (1 - row_y), half, 0)
    halo_far = lax.ppermute(halo_for, "az", across)

    v_sib, p_sib = to_sibling(velocity), to_sibling(pressure)
    far_sib, halo_sib, halo_far_sib = to_sibling(far), to_sibling(halo), to_sibling(halo_far)
    lags = lag_rows(info, velocity, v_sib, far, far_sib, halo, halo_sib, halo_far, halo_far_sib)

    up_sib, upper_sib, third_sib = to_sibling(up), to_sibling(upper), to_sibling(third)
    outs = products(
        info, offsets, lags,
        [pressure, up, far, upper, third, p_sib, up_sib, far_sib, upper_sib, third_sib],
    )
    parts = [outs[0]]
    for k in range(1, ta_n):
        parts.append(lax.ppermute(outs[k], "ta", [(i, i ^ k) for i in range(ta_n)]))
    return close(parts, factor, offsets.shape[0], azim)


def solution(mesh):
    return jax.shard_map(
        shards,
        mesh=mesh,
        in_specs=(P("gx", "az", "ta"), P("gx", "az", "ta"), P()),
        out_specs=P(("gx", "az", "ta"), None, None),
        check_vma=False,
    )
```

```python
import functools
import math

import jax
import jax.numpy as jnp
from jax import lax
from jax.experimental import pallas as pl
from jax.experimental.pallas import tpu as pltpu
from jax.sharding import PartitionSpec as P

MAXLAG = 16
LAGS = 2 * MAXLAG + 1
MAIN = 2 * MAXLAG
LANES = 128
BF16 = jnp.bfloat16
F32 = jnp.float32


def split(x):
    high = x.astype(BF16)
    return high, (x - high.astype(F32)).astype(BF16)


def in_core_order(core, mine, other):
    first = jnp.where(core == 0, mine, other)
    second = jnp.where(core == 0, other, mine)
    return jnp.concatenate([first, second], axis=0)


def fetch_kernel(info, velocity, out, part):
    half = part.shape[0]
    for i in range(half):
        part[i] = velocity[(1 - info[1]) * half + i]
    out[...] = velocity[...]


def lag_kernel(flip, info, v_own, v_sib, v_far, v_far_sib, h_near, h_away, out):
    core, row_y = info[0], info[1]
    rows, times = v_own.shape[1:]
    width = times + LANES
    for i in range(out.shape[0]):
        station = info[2] ^ (flip + 2 * i)
        near = (v_own, v_sib, h_near, info[3] + station, row_y)
        away = (v_far, v_far_sib, h_away, info[4] + station, 1 - row_y)
        for v_a, v_b, h, at_v, place in (near, away):
            series = in_core_order(core, v_a[at_v], v_b[at_v])
            series = jnp.concatenate([series, h[info[4] + station]], axis=1)
            for b in range(2 * rows):
                line = jnp.broadcast_to(series[b : b + 1, :], (8, width))
                for half in range(MAIN // 16):
                    parts = [
                        pltpu.roll(line, (8 * g - MAXLAG) % width, 1, stride=1, stride_axis=0)[:, :times]
                        for g in (2 * half, 2 * half + 1)
                    ]
                    high, low = split(jnp.concatenate(parts, axis=0))
                    at = b * MAIN + 16 * half
                    out[i, 0, place, at : at + 16, :] = high
                    out[i, 1, place, at : at + 16, :] = low
            high, low = split(pltpu.roll(series, MAXLAG, 1)[:, :times])
            at = 2 * rows * MAIN
            out[i, 0, place, at : at + 2 * rows, :] = high
            out[i, 1, place, at : at + 2 * rows, :] = low


def turn(x, by, azim):
    lane = lax.broadcasted_iota(jnp.int32, x.shape, 1) % azim
    left = pltpu.roll(x, LANES - by, 1)
    right = pltpu.roll(x, azim - by, 1)
    return jnp.where(lane < azim - by, left, right)


def window_kernel(info, o_own, u_own, o_far, u_far, o_sib, u_sib, o_far_sib, u_far_sib, high_p, low_p):
    core, row_y, last_gx = info[0], info[1], info[5]
    half = o_own.shape[0] // 2
    keep_up = jnp.where(last_gx == 1, 0.0, 1.0).astype(F32)
    keep_mid = jnp.where((last_gx == 1) & (row_y == 1), 0.0, 1.0).astype(F32)
    near = (o_own, u_own, o_sib, u_sib, row_y)
    away = (o_far, u_far, o_far_sib, u_far_sib, 1 - row_y)

    def one(w, carry):
        shift = row_y * half + w
        for o_a, u_a, o_b, u_b, at in (near, away):
            low_slot = in_core_order(core, o_a[shift], o_b[shift])
            middle = in_core_order(
                core,
                jnp.where(row_y == 0, o_a[half + w], u_a[w]),
                jnp.where(row_y == 0, o_b[half + w], u_b[w]),
            )
            high_slot = in_core_order(core, u_a[shift], u_b[shift])
            for slot, x in enumerate((low_slot, middle * keep_mid, high_slot * keep_up)):
                high, low = split(x)
                high_p[slot * half + w, at] = high
                low_p[slot * half + w, at] = low
        return carry

    lax.fori_loop(0, half, one, 0)


def product_kernel(flip, info, offsets, lags, high_p, low_p, out, prod):
    core, place = info[0], info[2]
    half = high_p.shape[0] // 3
    rows, azim = high_p.shape[2] // 2, 2 * high_p.shape[2]
    count = offsets.shape[0]
    for i in range(out.shape[0]):
        station = place ^ (flip + 2 * i)
        first = (half // 2) * core + station
        right = []
        for turned in (0, 1):
            tiles = {0: [], 1: []}
            for k in range(count):
                w = first + offsets[k]
                for which, source in ((0, high_p), (1, low_p)):
                    tiles[which] += [source[w, turned], source[w, 1 - turned]]
            high = jnp.concatenate(tiles[0], axis=0)
            low = jnp.concatenate(tiles[1], axis=0)
            right += [high, low, high]
        right = jnp.concatenate(right, axis=1)
        left = []
        for y in (0, 1):
            left += [lags[i, 0, y], lags[i, 0, y], lags[i, 1, y]]
        left = jnp.concatenate(left, axis=1)
        prod[i] = lax.dot_general(left, right, (((1,), (1,)), ((), ())), preferred_element_type=F32)
        out[i] = diagonals(prod.at[i], rows, azim, count)


def diagonals(prod, rows, azim, count):
    pieces = []
    for c in range(0, count * azim, LANES):
        level = [prod[b * MAIN : (b + 1) * MAIN, c : c + LANES] for b in range(2 * rows)]
        by = 1
        while len(level) > 1:
            level = [level[i] + turn(level[i + 1], by, azim) for i in range(0, len(level), 2)]
            by *= 2
        extra = prod[2 * rows * MAIN : 2 * rows * (MAIN + 1), c : c + LANES]
        row = lax.broadcasted_iota(jnp.int32, extra.shape, 0)
        by = 1
        while by < 2 * rows:
            extra = jnp.where((row & by) != 0, turn(extra, by, azim), extra)
            by *= 2
        tail = jnp.broadcast_to(jnp.sum(extra, axis=0, keepdims=True), (8, LANES))
        pieces.append(jnp.concatenate([level[0], tail], axis=0))
    return jnp.concatenate(pieces, axis=1)


def close_kernel(factor, count, azim, *refs):
    mine, first, second, out = refs
    total = (mine[0] + first[0] + second[...]) * factor
    groups = LANES // azim
    lane = lax.broadcasted_iota(jnp.int32, (count, LANES), 1) // azim
    sub = lax.broadcasted_iota(jnp.int32, (count, LANES), 0)
    for tile in range(-(-LAGS // groups)):
        acc = jnp.zeros((count, LANES), F32)
        for j in range(groups):
            tau = tile * groups + j
            if tau >= LAGS:
                continue
            x = jnp.zeros((count, LANES), F32)
            for part in range(count // groups):
                line = total[tau : tau + 1, part * LANES : (part + 1) * LANES]
                x = jnp.where(sub // groups == part, jnp.broadcast_to(line, (count, LANES)), x)
            moved = x
            for s in range(groups):
                by = ((j - s) * azim) % LANES
                shifted = pltpu.roll(x, by, 1) if by else x
                moved = jnp.where(sub % groups == s, shifted, moved)
            acc = jnp.where(lane == j, moved, acc)
        width = min(LANES, (LAGS - tile * groups) * azim)
        out[0, :, tile * LANES : tile * LANES + width] = acc[:, :width]


VMEM = pl.BlockSpec(memory_space=pltpu.VMEM)
SMEM = pl.BlockSpec(memory_space=pltpu.SMEM)


def fetch(info, velocity):
    shape = velocity.shape
    return pl.pallas_call(
        fetch_kernel,
        in_specs=[SMEM, VMEM],
        out_specs=[VMEM, VMEM],
        out_shape=[
            jax.ShapeDtypeStruct(shape, F32),
            jax.ShapeDtypeStruct((shape[0] // 2,) + shape[1:], F32),
        ],
        compiler_params=pltpu.CompilerParams(vmem_limit_bytes=2 << 20),
        cost_estimate=pl.CostEstimate(flops=0, bytes_accessed=1 << 19, transcendentals=0),
    )(info, velocity)


def lag_rows(flip, info, stations, *arrays):
    rows, times = arrays[0].shape[1:]
    shape = (stations, 2, 2, 2 * rows * (MAIN + 1), times)
    return pl.pallas_call(
        functools.partial(lag_kernel, flip),
        in_specs=[SMEM] + [VMEM] * len(arrays),
        out_specs=VMEM,
        out_shape=jax.ShapeDtypeStruct(shape, BF16),
        compiler_params=pltpu.CompilerParams(vmem_limit_bytes=12 << 20),
        cost_estimate=pl.CostEstimate(flops=10_000_000, bytes_accessed=3 << 20, transcendentals=0),
    )(info, *arrays)


def window(info, pieces):
    stations, rows, times = pieces[0].shape
    shape = jax.ShapeDtypeStruct((stations // 2 * 3, 2, 2 * rows, times), BF16)
    return pl.pallas_call(
        window_kernel,
        in_specs=[SMEM] + [VMEM] * len(pieces),
        out_specs=[VMEM, VMEM],
        out_shape=[shape, shape],
        compiler_params=pltpu.CompilerParams(vmem_limit_bytes=8 << 20),
        cost_estimate=pl.CostEstimate(flops=2_000_000, bytes_accessed=2 << 20, transcendentals=0),
    )(info, *pieces)


def products(flip, info, offsets, lags, high_p, low_p):
    stations, _, _, height, times = lags.shape
    columns = offsets.shape[0] * 2 * high_p.shape[2]
    return pl.pallas_call(
        functools.partial(product_kernel, flip),
        in_specs=[SMEM, SMEM, VMEM, VMEM, VMEM],
        out_specs=VMEM,
        out_shape=jax.ShapeDtypeStruct((stations, MAIN + 8, columns), F32),
        scratch_shapes=[pltpu.VMEM((stations, height, columns), F32)],
        compiler_params=pltpu.CompilerParams(vmem_limit_bytes=24 << 20),
        cost_estimate=pl.CostEstimate(
            flops=2 * 3 * stations * 2 * height * times * columns,
            bytes_accessed=4 << 20, transcendentals=0,
        ),
    )(info, offsets, lags, high_p, low_p)


def close(parts, factor, count, azim):
    return pl.pallas_call(
        functools.partial(close_kernel, factor, count, azim),
        in_specs=[VMEM] * len(parts),
        out_specs=VMEM,
        out_shape=jax.ShapeDtypeStruct((1, count, LAGS * azim), F32),
        compiler_params=pltpu.CompilerParams(vmem_limit_bytes=4 << 20),
        cost_estimate=pl.CostEstimate(flops=1_000_000, bytes_accessed=1 << 18, transcendentals=0),
    )(*parts)


def shards(velocity, pressure, offsets):
    sta, rows, times = velocity.shape
    gx_n, az_n, ta_n = (lax.axis_size(name) for name in ("gx", "az", "ta"))
    gx, az, ta = (lax.axis_index(name) for name in ("gx", "az", "ta"))
    assert az_n == 4 and ta_n == 4 and sta == az_n * ta_n
    half, mine = sta // 2, sta // az_n
    core, row_y = az % 2, az // 2
    azim = rows * az_n
    factor = 1.0 / math.sqrt(times * ta_n * azim)

    sibling = [(i, i ^ 1) for i in range(az_n)]
    across = [(i, i ^ 2) for i in range(az_n)]
    gx_az = [(g, a) for g in range(gx_n) for a in range(az_n)]
    flat = lambda g, a: (g % gx_n) * az_n + a
    upstream = [(g, (g - 1) % gx_n) for g in range(gx_n)]
    diagonal = [(flat(g, a), flat(g - 1, a ^ 2)) for g, a in gx_az]
    pairs = (
        [i ^ 1 if (i ^ 1) < ta_n else i for i in range(ta_n)],
        [min(max(((i + 1) ^ 1) - 1, 0), ta_n - 1) for i in range(ta_n)],
    )
    az_ta = [(a, t) for a in range(az_n) for t in range(ta_n)]
    in_time = [(a * ta_n + t, a * ta_n + pairs[a % 2][t]) for a, t in az_ta]
    in_time_across = [(a * ta_n + t, (a ^ 2) * ta_n + pairs[a % 2][t]) for a, t in az_ta]

    to_sibling = lambda x: lax.ppermute(x, "az", sibling)

    info = jnp.stack([
        core, row_y, ta, mine * az, mine * core, (gx == gx_n - 1).astype(jnp.int32),
    ]).astype(jnp.int32)

    diag = lax.ppermute(pressure, ("gx", "az"), diagonal)
    far = lax.ppermute(pressure, "az", across)
    vel, v_for = fetch(info, velocity)
    v_sib = to_sibling(velocity)
    v_far = lax.ppermute(v_for, "az", across)
    later, v_far = lax.optimization_barrier((pressure, v_far))
    up = lax.ppermute(later, "gx", upstream)

    even = ta % 2 == 0
    use_right = even == (core == 0)

    def edge(x):
        return jnp.where(use_right, x[:, :, times - LANES :], x[:, :, :LANES])

    edge_own, edge_sib = edge(vel), edge(v_sib)
    first_core = jnp.where(core == 0, edge_own, edge_sib)
    second_core = jnp.where(core == 0, edge_sib, edge_own)
    edges = jnp.concatenate([first_core, second_core], axis=1)
    ends = [lax.dynamic_slice_in_dim(edges, half * at, half, 0) for at in (row_y, 1 - row_y)]
    h_near = lax.ppermute(ends[0], ("az", "ta"), in_time)
    h_away = lax.ppermute(ends[1], ("az", "ta"), in_time_across)

    def halo(mine, other):
        got_a = jnp.where(core == 0, mine, other)
        got_b = jnp.where(core == 0, other, mine)
        before = jnp.where(even, got_b, got_a) * (ta > 0).astype(F32)
        after = jnp.where(even, got_a, got_b) * (ta < ta_n - 1).astype(F32)
        lane = lax.broadcasted_iota(jnp.int32, before.shape, before.ndim - 1)
        return jnp.where(lane < LANES // 2, after, before)

    v_far_sib = to_sibling(v_far)
    series = (vel, v_sib, v_far, v_far_sib, halo(h_near, to_sibling(h_near)), halo(h_away, to_sibling(h_away)))
    lags_give = lag_rows(1, info, ta_n // 2, *series)
    p_sib, up_sib, diag_sib, far_sib = (to_sibling(x) for x in (pressure, up, diag, far))
    lags_keep = lag_rows(0, info, ta_n // 2, *series)
    high_p, low_p = window(info, [pressure, up, far, diag, p_sib, up_sib, far_sib, diag_sib])

    give = products(1, info, offsets, lags_give, high_p, low_p)
    first = lax.ppermute(give, "ta", [(i, i ^ 1) for i in range(ta_n)])
    keep = products(0, info, offsets, lags_keep, high_p, low_p)
    second = lax.ppermute(keep[1] + first[1], "ta", [(i, i ^ 2) for i in range(ta_n)])
    return close([keep, first, second], factor, offsets.shape[0], azim)


def solution(mesh):
    return jax.shard_map(
        shards,
        mesh=mesh,
        in_specs=(P("gx", "az", "ta"), P("gx", "az", "ta"), P()),
        out_specs=P(("gx", "az", "ta"), None, None),
        check_vma=False,
    )
```

```python
import functools
import math

import jax
import jax.numpy as jnp
from jax import lax
from jax.experimental import pallas as pl
from jax.experimental.pallas import tpu as pltpu
from jax.sharding import PartitionSpec as P

MAXLAG = 16
LAGS = 2 * MAXLAG + 1
MAIN = 2 * MAXLAG
LANES = 128
BF16 = jnp.bfloat16
F32 = jnp.float32


def position():
    az, ta = lax.axis_index("az"), lax.axis_index("ta")
    return az, lax.rem(az, 2), lax.div(az, 2), ta


def split(x):
    high = x.astype(BF16)
    return high, (x - high.astype(F32)).astype(BF16)


def in_core_order(core, mine, other):
    first = jnp.where(core == 0, mine, other)
    second = jnp.where(core == 0, other, mine)
    return jnp.concatenate([first, second], axis=0)


def fetch_kernel(velocity, v_sib, out, part, ends_near, ends_away):
    half = part.shape[0]
    _, core, row_y, ta = position()
    right = lax.rem(ta + core, 2) == 0
    times = velocity.shape[2]
    for i in range(half):
        part[i] = velocity[(1 - row_y) * half + i]
    out[...] = velocity[...]
    lane = lax.broadcasted_iota(jnp.int32, ends_near.shape, 1) // MAXLAG
    for ends, first in ((ends_near, row_y * half), (ends_away, (1 - row_y) * half)):
        acc = jnp.zeros(ends.shape, F32)
        for j in range(half):
            def tile(lo):
                return in_core_order(core, velocity[first + j, :, lo : lo + LANES], v_sib[first + j, :, lo : lo + LANES])

            edge = jnp.where(right, pltpu.roll(tile(times - LANES), MAXLAG, 1), tile(0))
            edge = pltpu.roll(edge, MAXLAG * j, 1) if j else edge
            acc = jnp.where(lane == j, edge, acc)
        ends[...] = acc


def halo_tile(station, mine, other):
    _, core, _, ta = position()
    swap = lax.rem(ta + core, 2) == 0
    last = lax.axis_size("ta") - 1
    before = jnp.where(swap, other, mine) * jnp.where(ta == 0, 0.0, 1.0).astype(F32)
    after = jnp.where(swap, mine, other) * jnp.where(ta == last, 0.0, 1.0).astype(F32)
    start = lax.rem(LANES - MAXLAG * station, LANES)
    after = pltpu.roll(after, start, 1)
    before = pltpu.roll(before, lax.rem(start + LANES - MAXLAG, LANES), 1)
    lane = lax.broadcasted_iota(jnp.int32, after.shape, 1)
    return jnp.where(lane < LANES // 2, after, before)


def lag_kernel(flip, v_own, v_sib, v_far, v_far_sib, halos, halos_sib, out):
    az, core, row_y, place = position()
    rows, times = v_own.shape[1:]
    mine = v_own.shape[0] // lax.axis_size("az")
    width = times + LANES
    for i in range(out.shape[0]):
        station = place ^ (flip + 2 * i)
        in_chip = mine * core + station
        near = (v_own, v_sib, mine * az + station, row_y)
        away = (v_far, v_far_sib, in_chip, 1 - row_y)
        for which, (v_a, v_b, at_v, at) in enumerate((near, away)):
            series = in_core_order(core, v_a[at_v], v_b[at_v])
            edges = halo_tile(in_chip, halos[which], halos_sib[which])
            series = jnp.concatenate([series, edges], axis=1)
            for b in range(2 * rows):
                line = jnp.broadcast_to(series[b : b + 1, :], (8, width))
                for half in range(MAIN // 16):
                    parts = [
                        pltpu.roll(line, (8 * g - MAXLAG) % width, 1, stride=1, stride_axis=0)[:, :times]
                        for g in (2 * half, 2 * half + 1)
                    ]
                    high, low = split(jnp.concatenate(parts, axis=0))
                    row = b * MAIN + 16 * half
                    out[i, 0, at, row : row + 16, :] = high
                    out[i, 1, at, row : row + 16, :] = low
            high, low = split(pltpu.roll(series, MAXLAG, 1)[:, :times])
            row = 2 * rows * MAIN
            out[i, 0, at, row : row + 2 * rows, :] = high
            out[i, 1, at, row : row + 2 * rows, :] = low


def turn(x, by, azim):
    lane = lax.broadcasted_iota(jnp.int32, x.shape, 1) % azim
    left = pltpu.roll(x, LANES - by, 1)
    right = pltpu.roll(x, azim - by, 1)
    return jnp.where(lane < azim - by, left, right)


def window_kernel(o_own, u_own, o_far, u_far, o_sib, u_sib, o_far_sib, u_far_sib, high_p, low_p):
    _, core, row_y, _ = position()
    last_gx = lax.axis_index("gx") == lax.axis_size("gx") - 1
    half = o_own.shape[0] // 2
    keep_up = jnp.where(last_gx, 0.0, 1.0).astype(F32)
    keep_mid = jnp.where(last_gx & (row_y == 1), 0.0, 1.0).astype(F32)
    near = (o_own, u_own, o_sib, u_sib, row_y)
    away = (o_far, u_far, o_far_sib, u_far_sib, 1 - row_y)

    def one(w, carry):
        shift = row_y * half + w
        for o_a, u_a, o_b, u_b, at in (near, away):
            low_slot = in_core_order(core, o_a[shift], o_b[shift])
            middle = in_core_order(
                core,
                jnp.where(row_y == 0, o_a[half + w], u_a[w]),
                jnp.where(row_y == 0, o_b[half + w], u_b[w]),
            )
            high_slot = in_core_order(core, u_a[shift], u_b[shift])
            for slot, x in enumerate((low_slot, middle * keep_mid, high_slot * keep_up)):
                high, low = split(x)
                high_p[slot * half + w, at] = high
                low_p[slot * half + w, at] = low
        return carry

    lax.fori_loop(0, half, one, 0)


def product_kernel(flip, offsets, lags, high_p, low_p, out, prod):
    _, core, _, place = position()
    half = high_p.shape[0] // 3
    rows, azim = high_p.shape[2] // 2, 2 * high_p.shape[2]
    count = offsets.shape[1]
    for i in range(out.shape[0]):
        station = place ^ (flip + 2 * i)
        first = (half // 2) * core + station
        right = []
        for turned in (0, 1):
            tiles = {0: [], 1: []}
            for k in range(count):
                w = first + offsets[0, k]
                for which, source in ((0, high_p), (1, low_p)):
                    tiles[which] += [source[w, turned], source[w, 1 - turned]]
            high = jnp.concatenate(tiles[0], axis=0)
            low = jnp.concatenate(tiles[1], axis=0)
            right += [high, low, high]
        right = jnp.concatenate(right, axis=1)
        left = []
        for y in (0, 1):
            left += [lags[i, 0, y], lags[i, 0, y], lags[i, 1, y]]
        left = jnp.concatenate(left, axis=1)
        prod[i] = lax.dot_general(left, right, (((1,), (1,)), ((), ())), preferred_element_type=F32)
        out[i] = diagonals(prod.at[i], rows, azim, count)


def diagonals(prod, rows, azim, count):
    pieces = []
    for c in range(0, count * azim, LANES):
        level = [prod[b * MAIN : (b + 1) * MAIN, c : c + LANES] for b in range(2 * rows)]
        by = 1
        while len(level) > 1:
            level = [level[i] + turn(level[i + 1], by, azim) for i in range(0, len(level), 2)]
            by *= 2
        extra = prod[2 * rows * MAIN : 2 * rows * (MAIN + 1), c : c + LANES]
        row = lax.broadcasted_iota(jnp.int32, extra.shape, 0)
        by = 1
        while by < 2 * rows:
            extra = jnp.where((row & by) != 0, turn(extra, by, azim), extra)
            by *= 2
        tail = jnp.broadcast_to(jnp.sum(extra, axis=0, keepdims=True), (8, LANES))
        pieces.append(jnp.concatenate([level[0], tail], axis=0))
    return jnp.concatenate(pieces, axis=1)


def close_kernel(factor, count, azim, *refs):
    mine, first, second, out = refs
    total = (mine[0] + first[0] + second[...]) * factor
    groups = LANES // azim
    lane = lax.broadcasted_iota(jnp.int32, (count, LANES), 1) // azim
    sub = lax.broadcasted_iota(jnp.int32, (count, LANES), 0)
    for tile in range(-(-LAGS // groups)):
        acc = jnp.zeros((count, LANES), F32)
        for j in range(groups):
            tau = tile * groups + j
            if tau >= LAGS:
                continue
            x = jnp.zeros((count, LANES), F32)
            for part in range(count // groups):
                line = total[tau : tau + 1, part * LANES : (part + 1) * LANES]
                x = jnp.where(sub // groups == part, jnp.broadcast_to(line, (count, LANES)), x)
            moved = x
            for s in range(groups):
                by = ((j - s) * azim) % LANES
                shifted = pltpu.roll(x, by, 1) if by else x
                moved = jnp.where(sub % groups == s, shifted, moved)
            acc = jnp.where(lane == j, moved, acc)
        width = min(LANES, (LAGS - tile * groups) * azim)
        out[0, :, tile * LANES : tile * LANES + width] = acc[:, :width]


VMEM = pl.BlockSpec(memory_space=pltpu.VMEM)


def fetch(velocity, v_sib):
    stations, rows, times = velocity.shape
    shapes = [
        (stations, rows, times), (stations // 2, rows, times),
        (2 * rows, stations // 2 * MAXLAG), (2 * rows, stations // 2 * MAXLAG),
    ]
    return pl.pallas_call(
        fetch_kernel,
        in_specs=[VMEM, VMEM],
        out_specs=[VMEM] * len(shapes),
        out_shape=[jax.ShapeDtypeStruct(shape, F32) for shape in shapes],
        compiler_params=pltpu.CompilerParams(vmem_limit_bytes=2 << 20),
        cost_estimate=pl.CostEstimate(flops=0, bytes_accessed=1 << 19, transcendentals=0),
    )(velocity, v_sib)


def lag_rows(flip, stations, *arrays):
    rows, times = arrays[0].shape[1:]
    shape = (stations, 2, 2, 2 * rows * (MAIN + 1), times)
    return pl.pallas_call(
        functools.partial(lag_kernel, flip),
        in_specs=[VMEM] * len(arrays),
        out_specs=VMEM,
        out_shape=jax.ShapeDtypeStruct(shape, BF16),
        compiler_params=pltpu.CompilerParams(vmem_limit_bytes=12 << 20),
        cost_estimate=pl.CostEstimate(flops=10_000_000, bytes_accessed=3 << 20, transcendentals=0),
    )(*arrays)


def window(pieces):
    stations, rows, times = pieces[0].shape
    shape = jax.ShapeDtypeStruct((stations // 2 * 3, 2, 2 * rows, times), BF16)
    return pl.pallas_call(
        window_kernel,
        in_specs=[VMEM] * len(pieces),
        out_specs=[VMEM, VMEM],
        out_shape=[shape, shape],
        compiler_params=pltpu.CompilerParams(vmem_limit_bytes=8 << 20),
        cost_estimate=pl.CostEstimate(flops=2_000_000, bytes_accessed=2 << 20, transcendentals=0),
    )(*pieces)


def products(flip, offsets, lags, high_p, low_p):
    stations, _, _, height, times = lags.shape
    columns = offsets.shape[1] * 2 * high_p.shape[2]
    return pl.pallas_call(
        functools.partial(product_kernel, flip),
        in_specs=[VMEM] * 4,
        out_specs=VMEM,
        out_shape=jax.ShapeDtypeStruct((stations, MAIN + 8, columns), F32),
        scratch_shapes=[pltpu.VMEM((stations, height, columns), F32)],
        compiler_params=pltpu.CompilerParams(vmem_limit_bytes=24 << 20),
        cost_estimate=pl.CostEstimate(
            flops=2 * 3 * stations * 2 * height * times * columns,
            bytes_accessed=4 << 20, transcendentals=0,
        ),
    )(offsets, lags, high_p, low_p)


def close(parts, factor, count, azim):
    return pl.pallas_call(
        functools.partial(close_kernel, factor, count, azim),
        in_specs=[VMEM] * len(parts),
        out_specs=VMEM,
        out_shape=jax.ShapeDtypeStruct((1, count, LAGS * azim), F32),
        compiler_params=pltpu.CompilerParams(vmem_limit_bytes=4 << 20),
        cost_estimate=pl.CostEstimate(flops=1_000_000, bytes_accessed=1 << 18, transcendentals=0),
    )(*parts)


def shards(velocity, pressure, offsets):
    sta, rows, times = velocity.shape
    gx_n, az_n, ta_n = (lax.axis_size(name) for name in ("gx", "az", "ta"))
    assert az_n == 4 and ta_n == 4 and sta == az_n * ta_n
    azim = rows * az_n
    factor = 1.0 / math.sqrt(times * ta_n * azim)

    sibling = [(i, i ^ 1) for i in range(az_n)]
    across = [(i, i ^ 2) for i in range(az_n)]
    gx_az = [(g, a) for g in range(gx_n) for a in range(az_n)]
    flat = lambda g, a: (g % gx_n) * az_n + a
    upstream = [(g, (g - 1) % gx_n) for g in range(gx_n)]
    diagonal = [(flat(g, a), flat(g - 1, a ^ 2)) for g, a in gx_az]
    pairs = (
        [i ^ 1 if (i ^ 1) < ta_n else i for i in range(ta_n)],
        [min(max(((i + 1) ^ 1) - 1, 0), ta_n - 1) for i in range(ta_n)],
    )
    az_ta = [(a, t) for a in range(az_n) for t in range(ta_n)]
    in_time = [(a * ta_n + t, a * ta_n + pairs[a % 2][t]) for a, t in az_ta]
    in_time_across = [(a * ta_n + t, (a ^ 2) * ta_n + pairs[a % 2][t]) for a, t in az_ta]

    to_sibling = lambda x: lax.ppermute(x, "az", sibling)

    far = lax.ppermute(pressure, "az", across)
    up = lax.ppermute(pressure, "gx", upstream)
    diag = lax.ppermute(pressure, ("gx", "az"), diagonal)
    v_sib, p_sib = to_sibling(velocity), to_sibling(pressure)
    vel, v_for, ends_near, ends_away = fetch(velocity, v_sib)
    ends_near, ends_away, p_sib = lax.optimization_barrier((ends_near, ends_away, p_sib))
    v_far = lax.ppermute(v_for, "az", across)
    h_near = lax.ppermute(ends_near, ("az", "ta"), in_time)
    h_away = lax.ppermute(ends_away, ("az", "ta"), in_time_across)

    h_away, h_near, diag, up, far = lax.optimization_barrier((h_away, h_near, diag, up, far))
    halos = jnp.stack([h_near, h_away])
    halos_sib = to_sibling(halos)
    up_sib, diag_sib, far_sib = (to_sibling(x) for x in (up, diag, far))
    series = (vel, v_sib, v_far, to_sibling(v_far), halos, halos_sib)
    high_p, low_p = window([pressure, up, far, diag, p_sib, up_sib, far_sib, diag_sib])
    offsets = offsets.reshape(1, -1)
    give = products(1, offsets, lag_rows(1, ta_n // 2, *series), high_p, low_p)
    first = lax.ppermute(give, "ta", [(i, i ^ 1) for i in range(ta_n)])
    keep = products(0, offsets, lag_rows(0, ta_n // 2, *series), high_p, low_p)
    second = lax.ppermute(keep[1] + first[1], "ta", [(i, i ^ 2) for i in range(ta_n)])
    return close([keep, first, second], factor, offsets.shape[1], azim)


def solution(mesh):
    return jax.shard_map(
        shards,
        mesh=mesh,
        in_specs=(P("gx", "az", "ta"), P("gx", "az", "ta"), P()),
        out_specs=P(("gx", "az", "ta"), None, None),
        check_vma=False,
    )
```

```python
import functools
import math

import jax
import jax.numpy as jnp
from jax import lax
from jax.experimental import pallas as pl
from jax.experimental.pallas import tpu as pltpu
from jax.sharding import PartitionSpec as P

MAXLAG = 16
LAGS = 2 * MAXLAG + 1
MAIN = 2 * MAXLAG
LANES = 128
BF16 = jnp.bfloat16
F32 = jnp.float32


def position():
    az, ta = lax.axis_index("az"), lax.axis_index("ta")
    return az, lax.rem(az, 2), lax.div(az, 2), ta


def split(x):
    high = x.astype(BF16)
    return high, (x - high.astype(F32)).astype(BF16)


def in_core_order(core, mine, other):
    first = jnp.where(core == 0, mine, other)
    second = jnp.where(core == 0, other, mine)
    return jnp.concatenate([first, second], axis=0)


def fetch_kernel(velocity, v_sib, out, part, ends_near, ends_away):
    half = part.shape[0]
    _, core, row_y, ta = position()
    right = lax.rem(ta + core, 2) == 0
    times = velocity.shape[2]
    for i in range(half):
        part[i] = velocity[(1 - row_y) * half + i]
    out[...] = velocity[...]
    lane = lax.broadcasted_iota(jnp.int32, ends_near.shape, 1) // MAXLAG
    for ends, first in ((ends_near, row_y * half), (ends_away, (1 - row_y) * half)):
        acc = jnp.zeros(ends_near.shape, F32)
        for j in range(half):
            def tile(lo):
                return in_core_order(core, velocity[first + j, :, lo : lo + LANES], v_sib[first + j, :, lo : lo + LANES])

            edge = jnp.where(right, pltpu.roll(tile(times - LANES), MAXLAG, 1), tile(0))
            edge = pltpu.roll(edge, MAXLAG * j, 1) if j else edge
            acc = jnp.where(lane == j, edge, acc)
        ends[...] = acc


def halo_tile(station, mine, other):
    _, core, _, ta = position()
    swap = lax.rem(ta + core, 2) == 0
    last = lax.axis_size("ta") - 1
    before = jnp.where(swap, other, mine) * jnp.where(ta == 0, 0.0, 1.0).astype(F32)
    after = jnp.where(swap, mine, other) * jnp.where(ta == last, 0.0, 1.0).astype(F32)
    start = lax.rem(LANES - MAXLAG * station, LANES)
    after = pltpu.roll(after, start, 1)
    before = pltpu.roll(before, lax.rem(start + LANES - MAXLAG, LANES), 1)
    lane = lax.broadcasted_iota(jnp.int32, after.shape, 1)
    return jnp.where(lane < LANES // 2, after, before)


def lag_kernel(flips, away, v_a, v_b, h_a, h_b, out):
    az, core, row_y, place = position()
    rows, times = v_a.shape[1:]
    mine = lax.axis_size("ta")
    width = times + LANES
    for i in range(out.shape[0]):
        station = i if flips is None else place ^ flips[i]
        in_chip = mine * core + station
        at_v = in_chip if away else mine * az + station
        series = in_core_order(core, v_a[at_v], v_b[at_v])
        edges = halo_tile(in_chip, h_a[...], h_b[...])
        series = jnp.concatenate([series, edges], axis=1)
        for b in range(2 * rows):
            line = jnp.broadcast_to(series[b : b + 1, :], (8, width))
            for half in range(MAIN // 16):
                parts = [
                    pltpu.roll(line, (8 * g - MAXLAG) % width, 1, stride=1, stride_axis=0)[:, :times]
                    for g in (2 * half, 2 * half + 1)
                ]
                high, low = split(jnp.concatenate(parts, axis=0))
                row = b * MAIN + 16 * half
                out[i, 0, row : row + 16, :] = high
                out[i, 1, row : row + 16, :] = low
        high, low = split(pltpu.roll(series, MAXLAG, 1)[:, :times])
        row = 2 * rows * MAIN
        out[i, 0, row : row + 2 * rows, :] = high
        out[i, 1, row : row + 2 * rows, :] = low


def window_kernel(o_own, u_own, o_far, u_far, o_sib, u_sib, o_far_sib, u_far_sib, high_p, low_p):
    _, core, row_y, _ = position()
    last_gx = lax.axis_index("gx") == lax.axis_size("gx") - 1
    half = o_own.shape[0] // 2
    keep_up = jnp.where(last_gx, 0.0, 1.0).astype(F32)
    keep_mid = jnp.where(last_gx & (row_y == 1), 0.0, 1.0).astype(F32)
    near = (o_own, u_own, o_sib, u_sib, row_y)
    away = (o_far, u_far, o_far_sib, u_far_sib, 1 - row_y)

    def one(w, carry):
        shift = row_y * half + w
        for o_a, u_a, o_b, u_b, at in (near, away):
            low_slot = in_core_order(core, o_a[shift], o_b[shift])
            middle = in_core_order(
                core,
                jnp.where(row_y == 0, o_a[half + w], u_a[w]),
                jnp.where(row_y == 0, o_b[half + w], u_b[w]),
            )
            high_slot = in_core_order(core, u_a[shift], u_b[shift])
            for slot, x in enumerate((low_slot, middle * keep_mid, high_slot * keep_up)):
                high, low = split(x)
                high_p[slot * half + w, at] = high
                low_p[slot * half + w, at] = low
        return carry

    lax.fori_loop(0, half, one, 0)


def product_kernel(flips, offsets, lags_near, lags_away, high_p, low_p, out, prod):
    _, core, row_y, place = position()
    half = high_p.shape[0] // 3
    rows, azim = high_p.shape[2] // 2, 2 * high_p.shape[2]
    count = offsets.shape[1]
    for i, flip in enumerate(flips):
        station = place ^ flip
        first = (half // 2) * core + station
        right = []
        for turned in (row_y, 1 - row_y):
            tiles = {0: [], 1: []}
            for k in range(count):
                w = first + offsets[0, k]
                for which, source in ((0, high_p), (1, low_p)):
                    tiles[which] += [source[w, turned], source[w, 1 - turned]]
            high = jnp.concatenate(tiles[0], axis=0)
            low = jnp.concatenate(tiles[1], axis=0)
            right += [high, low, high]
        right = jnp.concatenate(right, axis=1)
        left = []
        for lags, at in ((lags_near, station), (lags_away, i)):
            left += [lags[at, 0], lags[at, 0], lags[at, 1]]
        left = jnp.concatenate(left, axis=1)
        prod[i] = lax.dot_general(left, right, (((1,), (1,)), ((), ())), preferred_element_type=F32)
        out[i] = diagonals(prod.at[i], rows, azim, count)


def diagonals(prod, rows, azim, count):
    lane = lax.broadcasted_iota(jnp.int32, (1, LANES), 1) % azim
    pieces = []
    for c in range(0, count * azim, LANES):
        inside = prod[:MAIN, c : c + LANES]
        beyond = jnp.zeros_like(inside)
        for b in range(1, 2 * rows):
            moved = pltpu.roll(prod[b * MAIN : (b + 1) * MAIN, c : c + LANES], LANES - b, 1)
            inside += jnp.where(lane < azim - b, moved, 0.0)
            beyond += jnp.where(lane < azim - b, 0.0, moved)
        extra = prod[2 * rows * MAIN : 2 * rows * (MAIN + 1), c : c + LANES]
        row = lax.broadcasted_iota(jnp.int32, extra.shape, 0)
        moved, by = extra, 1
        while by < 2 * rows:
            moved = jnp.where((row & by) != 0, pltpu.roll(moved, LANES - by, 1), moved)
            by *= 2
        ends = [
            jnp.broadcast_to(jnp.sum(jnp.where(keep, moved, 0.0), axis=0, keepdims=True), (8, LANES))
            for keep in (lane < azim - row, lane >= azim - row)
        ]
        inside = jnp.concatenate([inside, ends[0]], axis=0)
        beyond = jnp.concatenate([beyond, ends[1]], axis=0)
        pieces.append(inside + pltpu.roll(beyond, azim, 1))
    return jnp.concatenate(pieces, axis=1)


def close_kernel(factor, count, azim, *refs):
    mine, first, second, out = refs
    total = (mine[0] + first[0] + second[...]) * factor
    groups = LANES // azim
    lane = lax.broadcasted_iota(jnp.int32, (count, LANES), 1) // azim
    sub = lax.broadcasted_iota(jnp.int32, (count, LANES), 0)
    for tile in range(-(-LAGS // groups)):
        acc = jnp.zeros((count, LANES), F32)
        for j in range(groups):
            tau = tile * groups + j
            if tau >= LAGS:
                continue
            x = jnp.zeros((count, LANES), F32)
            for part in range(count // groups):
                line = total[tau : tau + 1, part * LANES : (part + 1) * LANES]
                x = jnp.where(sub // groups == part, jnp.broadcast_to(line, (count, LANES)), x)
            moved = x
            for s in range(groups):
                by = ((j - s) * azim) % LANES
                shifted = pltpu.roll(x, by, 1) if by else x
                moved = jnp.where(sub % groups == s, shifted, moved)
            acc = jnp.where(lane == j, moved, acc)
        width = min(LANES, (LAGS - tile * groups) * azim)
        out[0, :, tile * LANES : tile * LANES + width] = acc[:, :width]


VMEM = pl.BlockSpec(memory_space=pltpu.VMEM)


def fetch(velocity, v_sib):
    stations, rows, times = velocity.shape
    shapes = [
        (stations, rows, times), (stations // 2, rows, times),
        (2 * rows, stations // 2 * MAXLAG), (2 * rows, stations // 2 * MAXLAG),
    ]
    return pl.pallas_call(
        fetch_kernel,
        in_specs=[VMEM, VMEM],
        out_specs=[VMEM] * len(shapes),
        out_shape=[jax.ShapeDtypeStruct(shape, F32) for shape in shapes],
        compiler_params=pltpu.CompilerParams(vmem_limit_bytes=2 << 20),
        cost_estimate=pl.CostEstimate(flops=0, bytes_accessed=1 << 19, transcendentals=0),
    )(velocity, v_sib)


def lag_rows(flips, away, *arrays):
    rows, times = arrays[0].shape[1:]
    stations = lax.axis_size("ta") if flips is None else len(flips)
    shape = (stations, 2, 2 * rows * (MAIN + 1), times)
    return pl.pallas_call(
        functools.partial(lag_kernel, flips, away),
        in_specs=[VMEM] * len(arrays),
        out_specs=VMEM,
        out_shape=jax.ShapeDtypeStruct(shape, BF16),
        compiler_params=pltpu.CompilerParams(vmem_limit_bytes=12 << 20),
        cost_estimate=pl.CostEstimate(flops=10_000_000, bytes_accessed=3 << 20, transcendentals=0),
    )(*arrays)


def window(pieces):
    stations, rows, times = pieces[0].shape
    shape = jax.ShapeDtypeStruct((stations // 2 * 3, 2, 2 * rows, times), BF16)
    return pl.pallas_call(
        window_kernel,
        in_specs=[VMEM] * len(pieces),
        out_specs=[VMEM, VMEM],
        out_shape=[shape, shape],
        compiler_params=pltpu.CompilerParams(vmem_limit_bytes=8 << 20),
        cost_estimate=pl.CostEstimate(flops=2_000_000, bytes_accessed=2 << 20, transcendentals=0),
    )(*pieces)


def products(flips, offsets, near, away, high_p, low_p):
    stations, _, height, times = away.shape
    columns = offsets.shape[1] * 2 * high_p.shape[2]
    return pl.pallas_call(
        functools.partial(product_kernel, flips),
        in_specs=[VMEM] * 5,
        out_specs=VMEM,
        out_shape=jax.ShapeDtypeStruct((stations, MAIN + 8, columns), F32),
        scratch_shapes=[pltpu.VMEM((stations, height, columns), F32)],
        compiler_params=pltpu.CompilerParams(vmem_limit_bytes=24 << 20),
        cost_estimate=pl.CostEstimate(
            flops=2 * 3 * stations * 2 * height * times * columns,
            bytes_accessed=4 << 20, transcendentals=0,
        ),
    )(offsets, near, away, high_p, low_p)


def close(parts, factor, count, azim):
    return pl.pallas_call(
        functools.partial(close_kernel, factor, count, azim),
        in_specs=[VMEM] * len(parts),
        out_specs=VMEM,
        out_shape=jax.ShapeDtypeStruct((1, count, LAGS * azim), F32),
        compiler_params=pltpu.CompilerParams(vmem_limit_bytes=4 << 20),
        cost_estimate=pl.CostEstimate(flops=1_000_000, bytes_accessed=1 << 18, transcendentals=0),
    )(*parts)


def shards(velocity, pressure, offsets):
    sta, rows, times = velocity.shape
    gx_n, az_n, ta_n = (lax.axis_size(name) for name in ("gx", "az", "ta"))
    assert az_n == 4 and ta_n == 4 and sta == az_n * ta_n
    azim = rows * az_n
    factor = 1.0 / math.sqrt(times * ta_n * azim)

    sibling = [(i, i ^ 1) for i in range(az_n)]
    across = [(i, i ^ 2) for i in range(az_n)]
    gx_az = [(g, a) for g in range(gx_n) for a in range(az_n)]
    flat = lambda g, a: (g % gx_n) * az_n + a
    upstream = [(g, (g - 1) % gx_n) for g in range(gx_n)]
    diagonal = [(flat(g, a), flat(g - 1, a ^ 2)) for g, a in gx_az]
    pairs = (
        [i ^ 1 if (i ^ 1) < ta_n else i for i in range(ta_n)],
        [min(max(((i + 1) ^ 1) - 1, 0), ta_n - 1) for i in range(ta_n)],
    )
    az_ta = [(a, t) for a in range(az_n) for t in range(ta_n)]
    in_time = [(a * ta_n + t, a * ta_n + pairs[a % 2][t]) for a, t in az_ta]
    in_time_across = [(a * ta_n + t, (a ^ 2) * ta_n + pairs[a % 2][t]) for a, t in az_ta]

    to_sibling = lambda x: lax.ppermute(x, "az", sibling)

    far = lax.ppermute(pressure, "az", across)
    up = lax.ppermute(pressure, "gx", upstream)
    diag = lax.ppermute(pressure, ("gx", "az"), diagonal)
    v_sib, p_sib = to_sibling(velocity), to_sibling(pressure)
    vel, v_for, ends_near, ends_away = fetch(velocity, v_sib)
    ends_near, ends_away, p_sib = lax.optimization_barrier((ends_near, ends_away, p_sib))
    v_far = lax.ppermute(v_for, "az", across)
    h_near = lax.ppermute(ends_near, ("az", "ta"), in_time)
    h_away = lax.ppermute(ends_away, ("az", "ta"), in_time_across)
    h_away, h_near, diag, up, far = lax.optimization_barrier((h_away, h_near, diag, up, far))
    both = jnp.stack([h_near, h_away])
    both_sib = to_sibling(both)
    h_near_sib, h_away_sib = both_sib[0], both_sib[1]
    up_sib, diag_sib, far_sib, v_far_sib = (to_sibling(x) for x in (up, diag, far, v_far))
    near = lag_rows(None, False, vel, v_sib, h_near, h_near_sib)
    high_p, low_p = window([pressure, up, far, diag, p_sib, up_sib, far_sib, diag_sib])
    series = (v_far, v_far_sib, h_away, h_away_sib)

    offsets = offsets.reshape(1, -1)
    flips = (1, 3)
    give = products(flips, offsets, near, lag_rows(flips, True, *series), high_p, low_p)
    first = lax.ppermute(give, "ta", [(i, i ^ 1) for i in range(ta_n)])
    flips = (0, 2)
    keep = products(flips, offsets, near, lag_rows(flips, True, *series), high_p, low_p)
    second = lax.ppermute(keep[1] + first[1], "ta", [(i, i ^ 2) for i in range(ta_n)])
    return close([keep, first, second], factor, offsets.shape[1], azim)


def solution(mesh):
    return jax.shard_map(
        shards,
        mesh=mesh,
        in_specs=(P("gx", "az", "ta"), P("gx", "az", "ta"), P()),
        out_specs=P(("gx", "az", "ta"), None, None),
        check_vma=False,
    )
```

```python
import functools
import math

import jax
import jax.numpy as jnp
from jax import lax
from jax.experimental import pallas as pl
from jax.experimental.pallas import tpu as pltpu
from jax.sharding import PartitionSpec as P

MAXLAG = 16
LAGS = 2 * MAXLAG + 1
MAIN = 2 * MAXLAG
LANES = 128
BF16 = jnp.bfloat16
F32 = jnp.float32


def position():
    az, ta = lax.axis_index("az"), lax.axis_index("ta")
    return az, lax.rem(az, 2), lax.div(az, 2), ta


def split(x):
    high = x.astype(BF16)
    return high, (x - high.astype(F32)).astype(BF16)


def in_core_order(core, mine, other):
    first = jnp.where(core == 0, mine, other)
    second = jnp.where(core == 0, other, mine)
    return jnp.concatenate([first, second], axis=0)


def fetch_kernel(velocity, v_sib, out, part, ends_near, ends_away):
    half = part.shape[0]
    _, core, row_y, ta = position()
    right = lax.rem(ta + core, 2) == 0
    times = velocity.shape[2]
    for i in range(half):
        part[i] = velocity[(1 - row_y) * half + i]
    out[...] = velocity[...]
    lane = lax.broadcasted_iota(jnp.int32, ends_near.shape, 1) // MAXLAG
    for ends, first in ((ends_near, row_y * half), (ends_away, (1 - row_y) * half)):
        acc = jnp.zeros(ends_near.shape, F32)
        for j in range(half):
            def tile(lo):
                return in_core_order(core, velocity[first + j, :, lo : lo + LANES], v_sib[first + j, :, lo : lo + LANES])

            edge = jnp.where(right, pltpu.roll(tile(times - LANES), MAXLAG, 1), tile(0))
            edge = pltpu.roll(edge, MAXLAG * j, 1) if j else edge
            acc = jnp.where(lane == j, edge, acc)
        ends[...] = acc


def halo_tile(station, mine, other):
    _, core, _, ta = position()
    swap = lax.rem(ta + core, 2) == 0
    last = lax.axis_size("ta") - 1
    before = jnp.where(swap, other, mine) * jnp.where(ta == 0, 0.0, 1.0).astype(F32)
    after = jnp.where(swap, mine, other) * jnp.where(ta == last, 0.0, 1.0).astype(F32)
    start = lax.rem(LANES - MAXLAG * station, LANES)
    after = pltpu.roll(after, start, 1)
    before = pltpu.roll(before, lax.rem(start + LANES - MAXLAG, LANES), 1)
    lane = lax.broadcasted_iota(jnp.int32, after.shape, 1)
    return jnp.where(lane < LANES // 2, after, before)


def lag_kernel(flips, away, v_a, v_b, h_a, h_b, out):
    az, core, row_y, place = position()
    rows, times = v_a.shape[1:]
    mine = lax.axis_size("ta")
    width = times + LANES
    for i in range(out.shape[0]):
        station = i if flips is None else place ^ flips[i]
        in_chip = mine * core + station
        at_v = in_chip if away else mine * az + station
        series = in_core_order(core, v_a[at_v], v_b[at_v])
        edges = halo_tile(in_chip, h_a[...], h_b[...])
        series = jnp.concatenate([series, edges], axis=1)
        for b in range(2 * rows):
            line = jnp.broadcast_to(series[b : b + 1, :], (8, width))
            for half in range(MAIN // 16):
                parts = [
                    pltpu.roll(line, (8 * g - MAXLAG) % width, 1, stride=1, stride_axis=0)[:, :times]
                    for g in (2 * half, 2 * half + 1)
                ]
                high, low = split(jnp.concatenate(parts, axis=0))
                row = b * MAIN + 16 * half
                out[i, 0, row : row + 16, :] = high
                out[i, 1, row : row + 16, :] = low
        high, low = split(pltpu.roll(series, MAXLAG, 1)[:, :times])
        row = 2 * rows * MAIN
        out[i, 0, row : row + 2 * rows, :] = high
        out[i, 1, row : row + 2 * rows, :] = low


def window_kernel(o_own, u_own, o_far, u_far, o_sib, u_sib, o_far_sib, u_far_sib, high_p, low_p):
    _, core, row_y, _ = position()
    last_gx = lax.axis_index("gx") == lax.axis_size("gx") - 1
    half = o_own.shape[0] // 2
    keep_up = jnp.where(last_gx, 0.0, 1.0).astype(F32)
    keep_mid = jnp.where(last_gx & (row_y == 1), 0.0, 1.0).astype(F32)
    near = (o_own, u_own, o_sib, u_sib, row_y)
    away = (o_far, u_far, o_far_sib, u_far_sib, 1 - row_y)

    def one(w, carry):
        shift = row_y * half + w
        for o_a, u_a, o_b, u_b, at in (near, away):
            low_slot = in_core_order(core, o_a[shift], o_b[shift])
            middle = in_core_order(
                core,
                jnp.where(row_y == 0, o_a[half + w], u_a[w]),
                jnp.where(row_y == 0, o_b[half + w], u_b[w]),
            )
            high_slot = in_core_order(core, u_a[shift], u_b[shift])
            for slot, x in enumerate((low_slot, middle * keep_mid, high_slot * keep_up)):
                high, low = split(x)
                high_p[slot * half + w, at] = high
                low_p[slot * half + w, at] = low
        return carry

    lax.fori_loop(0, half, one, 0)


def product_kernel(flips, offsets, lags_near, lags_away, high_p, low_p, out, prod):
    _, core, row_y, place = position()
    half = high_p.shape[0] // 3
    rows, azim = high_p.shape[2] // 2, 2 * high_p.shape[2]
    count = offsets.shape[1]
    for i, flip in enumerate(flips):
        station = place ^ flip
        first = (half // 2) * core + station
        right = []
        for turned in (row_y, 1 - row_y):
            tiles = {0: [], 1: []}
            for k in range(count):
                w = first + offsets[0, k]
                for which, source in ((0, high_p), (1, low_p)):
                    tiles[which] += [source[w, turned], source[w, 1 - turned]]
            high = jnp.concatenate(tiles[0], axis=0)
            low = jnp.concatenate(tiles[1], axis=0)
            right += [high, low, high]
        right = jnp.concatenate(right, axis=1)
        left = []
        for lags, at in ((lags_near, i), (lags_away, i)):
            left += [lags[at, 0], lags[at, 0], lags[at, 1]]
        left = jnp.concatenate(left, axis=1)
        prod[i] = lax.dot_general(left, right, (((1,), (1,)), ((), ())), preferred_element_type=F32)
        out[i] = diagonals(prod.at[i], rows, azim, count)


def diagonals(prod, rows, azim, count):
    lane = lax.broadcasted_iota(jnp.int32, (1, LANES), 1) % azim
    pieces = []
    for c in range(0, count * azim, LANES):
        inside = prod[:MAIN, c : c + LANES]
        beyond = jnp.zeros_like(inside)
        for b in range(1, 2 * rows):
            moved = pltpu.roll(prod[b * MAIN : (b + 1) * MAIN, c : c + LANES], LANES - b, 1)
            inside += jnp.where(lane < azim - b, moved, 0.0)
            beyond += jnp.where(lane < azim - b, 0.0, moved)
        extra = prod[2 * rows * MAIN : 2 * rows * (MAIN + 1), c : c + LANES]
        row = lax.broadcasted_iota(jnp.int32, extra.shape, 0)
        moved, by = extra, 1
        while by < 2 * rows:
            moved = jnp.where((row & by) != 0, pltpu.roll(moved, LANES - by, 1), moved)
            by *= 2
        ends = [
            jnp.broadcast_to(jnp.sum(jnp.where(keep, moved, 0.0), axis=0, keepdims=True), (8, LANES))
            for keep in (lane < azim - row, lane >= azim - row)
        ]
        inside = jnp.concatenate([inside, ends[0]], axis=0)
        beyond = jnp.concatenate([beyond, ends[1]], axis=0)
        pieces.append(inside + pltpu.roll(beyond, azim, 1))
    return jnp.concatenate(pieces, axis=1)


def close_kernel(factor, count, azim, *refs):
    mine, first, second, out = refs
    total = (mine[0] + first[0] + second[...]) * factor
    groups = LANES // azim
    lane = lax.broadcasted_iota(jnp.int32, (count, LANES), 1) // azim
    sub = lax.broadcasted_iota(jnp.int32, (count, LANES), 0)
    for tile in range(-(-LAGS // groups)):
        acc = jnp.zeros((count, LANES), F32)
        for j in range(groups):
            tau = tile * groups + j
            if tau >= LAGS:
                continue
            x = jnp.zeros((count, LANES), F32)
            for part in range(count // groups):
                line = total[tau : tau + 1, part * LANES : (part + 1) * LANES]
                x = jnp.where(sub // groups == part, jnp.broadcast_to(line, (count, LANES)), x)
            moved = x
            for s in range(groups):
                by = ((j - s) * azim) % LANES
                shifted = pltpu.roll(x, by, 1) if by else x
                moved = jnp.where(sub % groups == s, shifted, moved)
            acc = jnp.where(lane == j, moved, acc)
        width = min(LANES, (LAGS - tile * groups) * azim)
        out[0, :, tile * LANES : tile * LANES + width] = acc[:, :width]


VMEM = pl.BlockSpec(memory_space=pltpu.VMEM)


def fetch(velocity, v_sib):
    stations, rows, times = velocity.shape
    shapes = [
        (stations, rows, times), (stations // 2, rows, times),
        (2 * rows, stations // 2 * MAXLAG), (2 * rows, stations // 2 * MAXLAG),
    ]
    return pl.pallas_call(
        fetch_kernel,
        in_specs=[VMEM, VMEM],
        out_specs=[VMEM] * len(shapes),
        out_shape=[jax.ShapeDtypeStruct(shape, F32) for shape in shapes],
        compiler_params=pltpu.CompilerParams(vmem_limit_bytes=2 << 20),
        cost_estimate=pl.CostEstimate(flops=0, bytes_accessed=1 << 19, transcendentals=0),
    )(velocity, v_sib)


def lag_rows(flips, away, *arrays):
    rows, times = arrays[0].shape[1:]
    stations = lax.axis_size("ta") if flips is None else len(flips)
    shape = (stations, 2, 2 * rows * (MAIN + 1), times)
    return pl.pallas_call(
        functools.partial(lag_kernel, flips, away),
        in_specs=[VMEM] * len(arrays),
        out_specs=VMEM,
        out_shape=jax.ShapeDtypeStruct(shape, BF16),
        compiler_params=pltpu.CompilerParams(vmem_limit_bytes=12 << 20),
        cost_estimate=pl.CostEstimate(flops=10_000_000, bytes_accessed=3 << 20, transcendentals=0),
    )(*arrays)


def window(pieces):
    stations, rows, times = pieces[0].shape
    shape = jax.ShapeDtypeStruct((stations // 2 * 3, 2, 2 * rows, times), BF16)
    return pl.pallas_call(
        window_kernel,
        in_specs=[VMEM] * len(pieces),
        out_specs=[VMEM, VMEM],
        out_shape=[shape, shape],
        compiler_params=pltpu.CompilerParams(vmem_limit_bytes=8 << 20),
        cost_estimate=pl.CostEstimate(flops=2_000_000, bytes_accessed=2 << 20, transcendentals=0),
    )(*pieces)


def products(flips, offsets, near, away, high_p, low_p):
    stations, _, height, times = away.shape
    columns = offsets.shape[1] * 2 * high_p.shape[2]
    return pl.pallas_call(
        functools.partial(product_kernel, flips),
        in_specs=[VMEM] * 5,
        out_specs=VMEM,
        out_shape=jax.ShapeDtypeStruct((stations, MAIN + 8, columns), F32),
        scratch_shapes=[pltpu.VMEM((stations, height, columns), F32)],
        compiler_params=pltpu.CompilerParams(vmem_limit_bytes=24 << 20),
        cost_estimate=pl.CostEstimate(
            flops=2 * 3 * stations * 2 * height * times * columns,
            bytes_accessed=4 << 20, transcendentals=0,
        ),
    )(offsets, near, away, high_p, low_p)


def close(parts, factor, count, azim):
    return pl.pallas_call(
        functools.partial(close_kernel, factor, count, azim),
        in_specs=[VMEM] * len(parts),
        out_specs=VMEM,
        out_shape=jax.ShapeDtypeStruct((1, count, LAGS * azim), F32),
        compiler_params=pltpu.CompilerParams(vmem_limit_bytes=4 << 20),
        cost_estimate=pl.CostEstimate(flops=1_000_000, bytes_accessed=1 << 18, transcendentals=0),
    )(*parts)


def shards(velocity, pressure, offsets):
    sta, rows, times = velocity.shape
    gx_n, az_n, ta_n = (lax.axis_size(name) for name in ("gx", "az", "ta"))
    assert az_n == 4 and ta_n == 4 and sta == az_n * ta_n
    azim = rows * az_n
    factor = 1.0 / math.sqrt(times * ta_n * azim)

    sibling = [(i, i ^ 1) for i in range(az_n)]
    across = [(i, i ^ 2) for i in range(az_n)]
    gx_az = [(g, a) for g in range(gx_n) for a in range(az_n)]
    flat = lambda g, a: (g % gx_n) * az_n + a
    upstream = [(g, (g - 1) % gx_n) for g in range(gx_n)]
    diagonal = [(flat(g, a), flat(g - 1, a ^ 2)) for g, a in gx_az]
    pairs = (
        [i ^ 1 if (i ^ 1) < ta_n else i for i in range(ta_n)],
        [min(max(((i + 1) ^ 1) - 1, 0), ta_n - 1) for i in range(ta_n)],
    )
    az_ta = [(a, t) for a in range(az_n) for t in range(ta_n)]
    in_time = [(a * ta_n + t, a * ta_n + pairs[a % 2][t]) for a, t in az_ta]
    in_time_across = [(a * ta_n + t, (a ^ 2) * ta_n + pairs[a % 2][t]) for a, t in az_ta]

    to_sibling = lambda x: lax.ppermute(x, "az", sibling)

    far = lax.ppermute(pressure, "az", across)
    up = lax.ppermute(pressure, "gx", upstream)
    diag = lax.ppermute(pressure, ("gx", "az"), diagonal)
    v_sib, p_sib = to_sibling(velocity), to_sibling(pressure)
    vel, v_for, ends_near, ends_away = fetch(velocity, v_sib)
    ends_near, ends_away, p_sib = lax.optimization_barrier((ends_near, ends_away, p_sib))
    v_far = lax.ppermute(v_for, "az", across)
    h_near = lax.ppermute(ends_near, ("az", "ta"), in_time)
    h_away = lax.ppermute(ends_away, ("az", "ta"), in_time_across)
    h_away, h_near, diag, up, far = lax.optimization_barrier((h_away, h_near, diag, up, far))
    both = jnp.stack([h_near, h_away])
    both_sib = to_sibling(both)
    h_near_sib, h_away_sib = both_sib[0], both_sib[1]
    up_sib, diag_sib, far_sib, v_far_sib = (to_sibling(x) for x in (up, diag, far, v_far))
    own = (vel, v_sib, h_near, h_near_sib)
    high_p, low_p = window([pressure, up, far, diag, p_sib, up_sib, far_sib, diag_sib])
    series = (v_far, v_far_sib, h_away, h_away_sib)

    offsets = offsets.reshape(1, -1)
    flips = (1, 3)
    give = products(flips, offsets, lag_rows(flips, False, *own), lag_rows(flips, True, *series), high_p, low_p)
    first = lax.ppermute(give, "ta", [(i, i ^ 1) for i in range(ta_n)])
    flips = (0, 2)
    keep = products(flips, offsets, lag_rows(flips, False, *own), lag_rows(flips, True, *series), high_p, low_p)
    second = lax.ppermute(keep[1] + first[1], "ta", [(i, i ^ 2) for i in range(ta_n)])
    return close([keep, first, second], factor, offsets.shape[1], azim)


def solution(mesh):
    return jax.shard_map(
        shards,
        mesh=mesh,
        in_specs=(P("gx", "az", "ta"), P("gx", "az", "ta"), P()),
        out_specs=P(("gx", "az", "ta"), None, None),
        check_vma=False,
    )
```

```python
import functools
import math

import jax
import jax.numpy as jnp
from jax import lax
from jax.experimental import pallas as pl
from jax.experimental.pallas import tpu as pltpu
from jax.sharding import PartitionSpec as P

MAXLAG = 16
LAGS = 2 * MAXLAG + 1
MAIN = 2 * MAXLAG
LANES = 128
BF16 = jnp.bfloat16
F32 = jnp.float32


def position():
    az, ta = lax.axis_index("az"), lax.axis_index("ta")
    return az, lax.rem(az, 2), lax.div(az, 2), ta


def split(x):
    high = x.astype(BF16)
    return high, (x - high.astype(F32)).astype(BF16)


def in_core_order(core, mine, other):
    first = jnp.where(core == 0, mine, other)
    second = jnp.where(core == 0, other, mine)
    return jnp.concatenate([first, second], axis=0)


def fetch_kernel(velocity, v_sib, out, part, ends_near, ends_away):
    half = part.shape[0]
    _, core, row_y, ta = position()
    right = lax.rem(ta + core, 2) == 0
    times = velocity.shape[2]
    for i in range(half):
        part[i] = velocity[(1 - row_y) * half + i]
    out[...] = velocity[...]
    lane = lax.broadcasted_iota(jnp.int32, ends_near.shape, 1) // MAXLAG
    for ends, first in ((ends_near, row_y * half), (ends_away, (1 - row_y) * half)):
        acc = jnp.zeros(ends_near.shape, F32)
        for j in range(half):
            def tile(lo):
                return in_core_order(core, velocity[first + j, :, lo : lo + LANES], v_sib[first + j, :, lo : lo + LANES])

            edge = jnp.where(right, pltpu.roll(tile(times - LANES), MAXLAG, 1), tile(0))
            edge = pltpu.roll(edge, MAXLAG * j, 1) if j else edge
            acc = jnp.where(lane == j, edge, acc)
        ends[...] = acc


def halo_tile(station, mine, other):
    _, core, _, ta = position()
    swap = lax.rem(ta + core, 2) == 0
    last = lax.axis_size("ta") - 1
    before = jnp.where(swap, other, mine) * jnp.where(ta == 0, 0.0, 1.0).astype(F32)
    after = jnp.where(swap, mine, other) * jnp.where(ta == last, 0.0, 1.0).astype(F32)
    start = lax.rem(LANES - MAXLAG * station, LANES)
    after = pltpu.roll(after, start, 1)
    before = pltpu.roll(before, lax.rem(start + LANES - MAXLAG, LANES), 1)
    lane = lax.broadcasted_iota(jnp.int32, after.shape, 1)
    return jnp.where(lane < LANES // 2, after, before)


def lag_kernel(flips, away, v_a, v_b, h_a, h_b, out):
    az, core, row_y, place = position()
    rows, times = v_a.shape[1:]
    mine = lax.axis_size("ta")
    width = times + LANES
    for i in range(out.shape[0]):
        station = i if flips is None else place ^ flips[i]
        in_chip = mine * core + station
        at_v = in_chip if away else mine * az + station
        series = in_core_order(core, v_a[at_v], v_b[at_v])
        edges = halo_tile(in_chip, h_a[...], h_b[...])
        series = jnp.concatenate([series, edges], axis=1)
        for b in range(2 * rows):
            line = jnp.broadcast_to(series[b : b + 1, :], (8, width))
            for half in range(MAIN // 16):
                parts = [
                    pltpu.roll(line, (8 * g - MAXLAG) % width, 1, stride=1, stride_axis=0)[:, :times]
                    for g in (2 * half, 2 * half + 1)
                ]
                high, low = split(jnp.concatenate(parts, axis=0))
                row = b * MAIN + 16 * half
                out[i, 0, row : row + 16, :] = high
                out[i, 1, row : row + 16, :] = low
        high, low = split(pltpu.roll(series, MAXLAG, 1)[:, :times])
        row = 2 * rows * MAIN
        out[i, 0, row : row + 2 * rows, :] = high
        out[i, 1, row : row + 2 * rows, :] = low


def window_kernel(o_own, u_own, o_far, u_far, o_sib, u_sib, o_far_sib, u_far_sib, high_p, low_p):
    _, core, row_y, _ = position()
    last_gx = lax.axis_index("gx") == lax.axis_size("gx") - 1
    half = o_own.shape[0] // 2
    keep_up = jnp.where(last_gx, 0.0, 1.0).astype(F32)
    keep_mid = jnp.where(last_gx & (row_y == 1), 0.0, 1.0).astype(F32)
    near = (o_own, u_own, o_sib, u_sib, row_y)
    away = (o_far, u_far, o_far_sib, u_far_sib, 1 - row_y)

    def one(w, carry):
        shift = row_y * half + w
        for o_a, u_a, o_b, u_b, at in (near, away):
            low_slot = in_core_order(core, o_a[shift], o_b[shift])
            middle = in_core_order(
                core,
                jnp.where(row_y == 0, o_a[half + w], u_a[w]),
                jnp.where(row_y == 0, o_b[half + w], u_b[w]),
            )
            high_slot = in_core_order(core, u_a[shift], u_b[shift])
            for slot, x in enumerate((low_slot, middle * keep_mid, high_slot * keep_up)):
                high, low = split(x)
                high_p[slot * half + w, at] = high
                low_p[slot * half + w, at] = low
        return carry

    lax.fori_loop(0, half, one, 0)


def product_kernel(flips, offsets, lags_near, lags_away, high_p, low_p, out, prod):
    _, core, row_y, place = position()
    half = high_p.shape[0] // 3
    rows, azim = high_p.shape[2] // 2, 2 * high_p.shape[2]
    count = offsets.shape[1]
    for i, flip in enumerate(flips):
        station = place ^ flip
        first = (half // 2) * core + station
        right = []
        for turned in (row_y, 1 - row_y):
            tiles = {0: [], 1: []}
            for k in range(count):
                w = first + offsets[0, k]
                for which, source in ((0, high_p), (1, low_p)):
                    tiles[which] += [source[w, turned], source[w, 1 - turned]]
            high = jnp.concatenate(tiles[0], axis=0)
            low = jnp.concatenate(tiles[1], axis=0)
            right += [high, low, high]
        right = jnp.concatenate(right, axis=1)
        left = []
        for lags, at in ((lags_near, i), (lags_away, i)):
            left += [lags[at, 0], lags[at, 0], lags[at, 1]]
        left = jnp.concatenate(left, axis=1)
        prod[i] = lax.dot_general(left, right, (((1,), (1,)), ((), ())), preferred_element_type=F32)
        out[i] = diagonals(prod.at[i], rows, azim, count)


def diagonals(prod, rows, azim, count):
    lane = lax.broadcasted_iota(jnp.int32, (1, LANES), 1) % azim
    pieces = []
    for c in range(0, count * azim, LANES):
        inside = prod[:MAIN, c : c + LANES]
        beyond = jnp.zeros_like(inside)
        for b in range(1, 2 * rows):
            moved = pltpu.roll(prod[b * MAIN : (b + 1) * MAIN, c : c + LANES], LANES - b, 1)
            inside += jnp.where(lane < azim - b, moved, 0.0)
            beyond += jnp.where(lane < azim - b, 0.0, moved)
        extra = prod[2 * rows * MAIN : 2 * rows * (MAIN + 1), c : c + LANES]
        row = lax.broadcasted_iota(jnp.int32, extra.shape, 0)
        moved, by = extra, 1
        while by < 2 * rows:
            moved = jnp.where((row & by) != 0, pltpu.roll(moved, LANES - by, 1), moved)
            by *= 2
        ends = [
            jnp.broadcast_to(jnp.sum(jnp.where(keep, moved, 0.0), axis=0, keepdims=True), (8, LANES))
            for keep in (lane < azim - row, lane >= azim - row)
        ]
        inside = jnp.concatenate([inside, ends[0]], axis=0)
        beyond = jnp.concatenate([beyond, ends[1]], axis=0)
        pieces.append(inside + pltpu.roll(beyond, azim, 1))
    return jnp.concatenate(pieces, axis=1)


def close_kernel(factor, count, azim, *refs):
    mine, first, second, out = refs
    total = (mine[0] + first[0] + second[...]) * factor
    groups = LANES // azim
    lane = lax.broadcasted_iota(jnp.int32, (count, LANES), 1) // azim
    sub = lax.broadcasted_iota(jnp.int32, (count, LANES), 0)
    for tile in range(-(-LAGS // groups)):
        acc = jnp.zeros((count, LANES), F32)
        for j in range(groups):
            tau = tile * groups + j
            if tau >= LAGS:
                continue
            x = jnp.zeros((count, LANES), F32)
            for part in range(count // groups):
                line = total[tau : tau + 1, part * LANES : (part + 1) * LANES]
                x = jnp.where(sub // groups == part, jnp.broadcast_to(line, (count, LANES)), x)
            moved = x
            for s in range(groups):
                by = ((j - s) * azim) % LANES
                shifted = pltpu.roll(x, by, 1) if by else x
                moved = jnp.where(sub % groups == s, shifted, moved)
            acc = jnp.where(lane == j, moved, acc)
        width = min(LANES, (LAGS - tile * groups) * azim)
        out[0, :, tile * LANES : tile * LANES + width] = acc[:, :width]


VMEM = pl.BlockSpec(memory_space=pltpu.VMEM)


def fetch(velocity, v_sib):
    stations, rows, times = velocity.shape
    shapes = [
        (stations, rows, times), (stations // 2, rows, times),
        (2 * rows, stations // 2 * MAXLAG), (2 * rows, stations // 2 * MAXLAG),
    ]
    return pl.pallas_call(
        fetch_kernel,
        in_specs=[VMEM, VMEM],
        out_specs=[VMEM] * len(shapes),
        out_shape=[jax.ShapeDtypeStruct(shape, F32) for shape in shapes],
        compiler_params=pltpu.CompilerParams(vmem_limit_bytes=2 << 20),
        cost_estimate=pl.CostEstimate(flops=0, bytes_accessed=1 << 19, transcendentals=0),
    )(velocity, v_sib)


def lag_rows(flips, away, *arrays):
    rows, times = arrays[0].shape[1:]
    stations = lax.axis_size("ta") if flips is None else len(flips)
    shape = (stations, 2, 2 * rows * (MAIN + 1), times)
    return pl.pallas_call(
        functools.partial(lag_kernel, flips, away),
        in_specs=[VMEM] * len(arrays),
        out_specs=VMEM,
        out_shape=jax.ShapeDtypeStruct(shape, BF16),
        compiler_params=pltpu.CompilerParams(vmem_limit_bytes=12 << 20),
        cost_estimate=pl.CostEstimate(flops=10_000_000, bytes_accessed=3 << 20, transcendentals=0),
    )(*arrays)


def window(pieces):
    stations, rows, times = pieces[0].shape
    shape = jax.ShapeDtypeStruct((stations // 2 * 3, 2, 2 * rows, times), BF16)
    return pl.pallas_call(
        window_kernel,
        in_specs=[VMEM] * len(pieces),
        out_specs=[VMEM, VMEM],
        out_shape=[shape, shape],
        compiler_params=pltpu.CompilerParams(vmem_limit_bytes=8 << 20),
        cost_estimate=pl.CostEstimate(flops=2_000_000, bytes_accessed=2 << 20, transcendentals=0),
    )(*pieces)


def products(flips, offsets, near, away, high_p, low_p):
    stations, _, height, times = away.shape
    columns = offsets.shape[1] * 2 * high_p.shape[2]
    return pl.pallas_call(
        functools.partial(product_kernel, flips),
        in_specs=[VMEM] * 5,
        out_specs=VMEM,
        out_shape=jax.ShapeDtypeStruct((stations, MAIN + 8, columns), F32),
        scratch_shapes=[pltpu.VMEM((stations, height, columns), F32)],
        compiler_params=pltpu.CompilerParams(vmem_limit_bytes=24 << 20),
        cost_estimate=pl.CostEstimate(
            flops=2 * 3 * stations * 2 * height * times * columns,
            bytes_accessed=4 << 20, transcendentals=0,
        ),
    )(offsets, near, away, high_p, low_p)


def close(parts, factor, count, azim):
    return pl.pallas_call(
        functools.partial(close_kernel, factor, count, azim),
        in_specs=[VMEM] * len(parts),
        out_specs=VMEM,
        out_shape=jax.ShapeDtypeStruct((1, count, LAGS * azim), F32),
        compiler_params=pltpu.CompilerParams(vmem_limit_bytes=4 << 20),
        cost_estimate=pl.CostEstimate(flops=1_000_000, bytes_accessed=1 << 18, transcendentals=0),
    )(*parts)


def shards(velocity, pressure, offsets):
    sta, rows, times = velocity.shape
    gx_n, az_n, ta_n = (lax.axis_size(name) for name in ("gx", "az", "ta"))
    assert az_n == 4 and ta_n == 4 and sta == az_n * ta_n
    azim = rows * az_n
    factor = 1.0 / math.sqrt(times * ta_n * azim)

    sibling = [(i, i ^ 1) for i in range(az_n)]
    across = [(i, i ^ 2) for i in range(az_n)]
    gx_az = [(g, a) for g in range(gx_n) for a in range(az_n)]
    flat = lambda g, a: (g % gx_n) * az_n + a
    upstream = [(g, (g - 1) % gx_n) for g in range(gx_n)]
    diagonal = [(flat(g, a), flat(g - 1, a ^ 2)) for g, a in gx_az]
    pairs = (
        [i ^ 1 if (i ^ 1) < ta_n else i for i in range(ta_n)],
        [min(max(((i + 1) ^ 1) - 1, 0), ta_n - 1) for i in range(ta_n)],
    )
    az_ta = [(a, t) for a in range(az_n) for t in range(ta_n)]
    in_time = [(a * ta_n + t, a * ta_n + pairs[a % 2][t]) for a, t in az_ta]
    in_time_across = [(a * ta_n + t, (a ^ 2) * ta_n + pairs[a % 2][t]) for a, t in az_ta]

    to_sibling = lambda x: lax.ppermute(x, "az", sibling)

    diag = lax.ppermute(pressure, ("gx", "az"), diagonal)
    far = lax.ppermute(pressure, "az", across)
    p_sib = to_sibling(pressure)
    v_sib = to_sibling(velocity)
    up = lax.ppermute(pressure, "gx", upstream)
    vel, v_for, ends_near, ends_away = fetch(velocity, v_sib)
    ends_near, ends_away = lax.optimization_barrier((ends_near, ends_away))
    h_near = lax.ppermute(ends_near, ("az", "ta"), in_time)
    v_far = lax.ppermute(v_for, "az", across)
    h_away = lax.ppermute(ends_away, ("az", "ta"), in_time_across)
    diag, h_away, h_near, up, far = lax.optimization_barrier((diag, h_away, h_near, up, far))
    both = jnp.stack([h_near, h_away])
    v_far, far = lax.optimization_barrier((v_far, far))
    up_sib = to_sibling(up)
    v_far_sib = to_sibling(v_far)
    diag_sib = to_sibling(diag)
    far_sib = to_sibling(far)
    both_sib = to_sibling(both)
    h_near_sib, h_away_sib = both_sib[0], both_sib[1]
    own = (vel, v_sib, h_near, h_near_sib)
    high_p, low_p = window([pressure, up, far, diag, p_sib, up_sib, far_sib, diag_sib])
    series = (v_far, v_far_sib, h_away, h_away_sib)

    offsets = offsets.reshape(1, -1)
    flips = (1, 3)
    give = products(flips, offsets, lag_rows(flips, False, *own), lag_rows(flips, True, *series), high_p, low_p)
    first = lax.ppermute(give, "ta", [(i, i ^ 1) for i in range(ta_n)])
    flips = (0, 2)
    keep = [
        products((flip,), offsets, lag_rows((flip,), False, *own), lag_rows((flip,), True, *series), high_p, low_p)
        for flip in (2, 0)
    ]
    second = lax.ppermute(keep[0][0] + first[1], "ta", [(i, i ^ 2) for i in range(ta_n)])
    return close([keep[1], first, second], factor, offsets.shape[1], azim)


def solution(mesh):
    return jax.shard_map(
        shards,
        mesh=mesh,
        in_specs=(P("gx", "az", "ta"), P("gx", "az", "ta"), P()),
        out_specs=P(("gx", "az", "ta"), None, None),
        check_vma=False,
    )
```

```python
import functools
import math

import jax
import jax.numpy as jnp
from jax import lax
from jax.experimental import pallas as pl
from jax.experimental.pallas import tpu as pltpu
from jax.sharding import PartitionSpec as P

MAXLAG = 16
LAGS = 2 * MAXLAG + 1
MAIN = 2 * MAXLAG
LANES = 128
BF16 = jnp.bfloat16
F32 = jnp.float32


def position():
    az, ta = lax.axis_index("az"), lax.axis_index("ta")
    return az, lax.rem(az, 2), lax.div(az, 2), ta


def split(x):
    high = x.astype(BF16)
    return high, (x - high.astype(F32)).astype(BF16)


def in_core_order(core, mine, other):
    first = jnp.where(core == 0, mine, other)
    second = jnp.where(core == 0, other, mine)
    return jnp.concatenate([first, second], axis=0)


def fetch_kernel(velocity, v_sib, out, part, ends_near, ends_away):
    half = part.shape[0]
    _, core, row_y, ta = position()
    right = lax.rem(ta + core, 2) == 0
    times = velocity.shape[2]
    for i in range(half):
        part[i] = velocity[(1 - row_y) * half + i]
    out[...] = velocity[...]
    lane = lax.broadcasted_iota(jnp.int32, ends_near.shape, 1) // MAXLAG
    for ends, first in ((ends_near, row_y * half), (ends_away, (1 - row_y) * half)):
        acc = jnp.zeros(ends_near.shape, F32)
        for j in range(half):
            def tile(lo):
                return in_core_order(core, velocity[first + j, :, lo : lo + LANES], v_sib[first + j, :, lo : lo + LANES])

            edge = jnp.where(right, pltpu.roll(tile(times - LANES), MAXLAG, 1), tile(0))
            edge = pltpu.roll(edge, MAXLAG * j, 1) if j else edge
            acc = jnp.where(lane == j, edge, acc)
        ends[...] = acc


def halo_tile(station, mine, other):
    _, core, _, ta = position()
    swap = lax.rem(ta + core, 2) == 0
    last = lax.axis_size("ta") - 1
    before = jnp.where(swap, other, mine) * jnp.where(ta == 0, 0.0, 1.0).astype(F32)
    after = jnp.where(swap, mine, other) * jnp.where(ta == last, 0.0, 1.0).astype(F32)
    start = lax.rem(LANES - MAXLAG * station, LANES)
    after = pltpu.roll(after, start, 1)
    before = pltpu.roll(before, lax.rem(start + LANES - MAXLAG, LANES), 1)
    lane = lax.broadcasted_iota(jnp.int32, after.shape, 1)
    return jnp.where(lane < LANES // 2, after, before)


def lag_kernel(flips, away, v_a, v_b, h_a, h_b, out):
    az, core, row_y, place = position()
    rows, times = v_a.shape[1:]
    mine = lax.axis_size("ta")
    width = times + LANES
    for i in range(out.shape[0]):
        station = i if flips is None else place ^ flips[i]
        in_chip = mine * core + station
        at_v = in_chip if away else mine * az + station
        series = in_core_order(core, v_a[at_v], v_b[at_v])
        edges = halo_tile(in_chip, h_a[...], h_b[...])
        series = jnp.concatenate([series, edges], axis=1)
        for b in range(2 * rows):
            line = jnp.broadcast_to(series[b : b + 1, :], (8, width))
            for half in range(MAIN // 16):
                parts = [
                    pltpu.roll(line, (8 * g - MAXLAG) % width, 1, stride=1, stride_axis=0)[:, :times]
                    for g in (2 * half, 2 * half + 1)
                ]
                high, low = split(jnp.concatenate(parts, axis=0))
                row = b * MAIN + 16 * half
                out[i, 0, row : row + 16, :] = high
                out[i, 1, row : row + 16, :] = low
        high, low = split(pltpu.roll(series, MAXLAG, 1)[:, :times])
        row = 2 * rows * MAIN
        out[i, 0, row : row + 2 * rows, :] = high
        out[i, 1, row : row + 2 * rows, :] = low


def window_kernel(o_own, u_own, o_far, u_far, o_sib, u_sib, o_far_sib, u_far_sib, high_p, low_p):
    _, core, row_y, _ = position()
    last_gx = lax.axis_index("gx") == lax.axis_size("gx") - 1
    half = o_own.shape[0] // 2
    keep_up = jnp.where(last_gx, 0.0, 1.0).astype(F32)
    keep_mid = jnp.where(last_gx & (row_y == 1), 0.0, 1.0).astype(F32)
    near = (o_own, u_own, o_sib, u_sib, row_y)
    away = (o_far, u_far, o_far_sib, u_far_sib, 1 - row_y)

    def one(w, carry):
        shift = row_y * half + w
        for o_a, u_a, o_b, u_b, at in (near, away):
            low_slot = in_core_order(core, o_a[shift], o_b[shift])
            middle = in_core_order(
                core,
                jnp.where(row_y == 0, o_a[half + w], u_a[w]),
                jnp.where(row_y == 0, o_b[half + w], u_b[w]),
            )
            high_slot = in_core_order(core, u_a[shift], u_b[shift])
            for slot, x in enumerate((low_slot, middle * keep_mid, high_slot * keep_up)):
                high, low = split(x)
                high_p[slot * half + w, at] = high
                low_p[slot * half + w, at] = low
        return carry

    lax.fori_loop(0, half, one, 0)


def product_kernel(flips, offsets, lags_near, lags_away, high_p, low_p, out, prod):
    _, core, row_y, place = position()
    half = high_p.shape[0] // 3
    rows, azim = high_p.shape[2] // 2, 2 * high_p.shape[2]
    count = offsets.shape[1]
    for i, flip in enumerate(flips):
        station = place ^ flip
        first = (half // 2) * core + station
        right = []
        for turned in (row_y, 1 - row_y):
            tiles = {0: [], 1: []}
            for k in range(count):
                w = first + offsets[0, k]
                for which, source in ((0, high_p), (1, low_p)):
                    tiles[which] += [source[w, turned], source[w, 1 - turned]]
            high = jnp.concatenate(tiles[0], axis=0)
            low = jnp.concatenate(tiles[1], axis=0)
            right += [high, low, high]
        right = jnp.concatenate(right, axis=1)
        left = []
        for lags, at in ((lags_near, i), (lags_away, i)):
            left += [lags[at, 0], lags[at, 0], lags[at, 1]]
        left = jnp.concatenate(left, axis=1)
        prod[i] = lax.dot_general(left, right, (((1,), (1,)), ((), ())), preferred_element_type=F32)
        sums = diagonals(prod.at[i], rows, azim, count)
        out[i * MAIN : (i + 1) * MAIN] = sums[:MAIN]
        end = sums[MAIN:]
        tail = end if i == 0 else jnp.where(lax.broadcasted_iota(jnp.int32, end.shape, 0) < i, tail, end)
    out[len(flips) * MAIN :] = tail


def diagonals(prod, rows, azim, count):
    lane = lax.broadcasted_iota(jnp.int32, (1, LANES), 1) % azim
    pieces = []
    for c in range(0, count * azim, LANES):
        inside = prod[:MAIN, c : c + LANES]
        beyond = jnp.zeros_like(inside)
        for b in range(1, 2 * rows):
            moved = pltpu.roll(prod[b * MAIN : (b + 1) * MAIN, c : c + LANES], LANES - b, 1)
            inside += jnp.where(lane < azim - b, moved, 0.0)
            beyond += jnp.where(lane < azim - b, 0.0, moved)
        extra = prod[2 * rows * MAIN : 2 * rows * (MAIN + 1), c : c + LANES]
        row = lax.broadcasted_iota(jnp.int32, extra.shape, 0)
        moved, by = extra, 1
        while by < 2 * rows:
            moved = jnp.where((row & by) != 0, pltpu.roll(moved, LANES - by, 1), moved)
            by *= 2
        ends = [
            jnp.broadcast_to(jnp.sum(jnp.where(keep, moved, 0.0), axis=0, keepdims=True), (8, LANES))
            for keep in (lane < azim - row, lane >= azim - row)
        ]
        inside = jnp.concatenate([inside, ends[0]], axis=0)
        beyond = jnp.concatenate([beyond, ends[1]], axis=0)
        pieces.append(inside + pltpu.roll(beyond, azim, 1))
    return jnp.concatenate(pieces, axis=1)


def close_kernel(factor, count, azim, *refs):
    mine, first, second, out = refs
    total = (mine[:MAIN] + first[:MAIN] + second[:MAIN]) * factor
    last = 2 * MAIN
    tail = (mine[MAIN : MAIN + 1] + first[last : last + 1] + second[MAIN + 1 : MAIN + 2]) * factor
    groups = LANES // azim
    lane = lax.broadcasted_iota(jnp.int32, (count, LANES), 1) // azim
    sub = lax.broadcasted_iota(jnp.int32, (count, LANES), 0)
    for tile in range(-(-LAGS // groups)):
        acc = jnp.zeros((count, LANES), F32)
        for j in range(groups):
            tau = tile * groups + j
            if tau >= LAGS:
                continue
            x = jnp.zeros((count, LANES), F32)
            for part in range(count // groups):
                source = total[tau : tau + 1] if tau < MAIN else tail
                line = source[:, part * LANES : (part + 1) * LANES]
                x = jnp.where(sub // groups == part, jnp.broadcast_to(line, (count, LANES)), x)
            moved = x
            for s in range(groups):
                by = ((j - s) * azim) % LANES
                shifted = pltpu.roll(x, by, 1) if by else x
                moved = jnp.where(sub % groups == s, shifted, moved)
            acc = jnp.where(lane == j, moved, acc)
        width = min(LANES, (LAGS - tile * groups) * azim)
        out[0, :, tile * LANES : tile * LANES + width] = acc[:, :width]


VMEM = pl.BlockSpec(memory_space=pltpu.VMEM)


def fetch(velocity, v_sib):
    stations, rows, times = velocity.shape
    shapes = [
        (stations, rows, times), (stations // 2, rows, times),
        (2 * rows, stations // 2 * MAXLAG), (2 * rows, stations // 2 * MAXLAG),
    ]
    return pl.pallas_call(
        fetch_kernel,
        in_specs=[VMEM, VMEM],
        out_specs=[VMEM] * len(shapes),
        out_shape=[jax.ShapeDtypeStruct(shape, F32) for shape in shapes],
        compiler_params=pltpu.CompilerParams(vmem_limit_bytes=2 << 20),
        cost_estimate=pl.CostEstimate(flops=0, bytes_accessed=1 << 19, transcendentals=0),
    )(velocity, v_sib)


def lag_rows(flips, away, *arrays):
    rows, times = arrays[0].shape[1:]
    stations = lax.axis_size("ta") if flips is None else len(flips)
    shape = (stations, 2, 2 * rows * (MAIN + 1), times)
    return pl.pallas_call(
        functools.partial(lag_kernel, flips, away),
        in_specs=[VMEM] * len(arrays),
        out_specs=VMEM,
        out_shape=jax.ShapeDtypeStruct(shape, BF16),
        compiler_params=pltpu.CompilerParams(vmem_limit_bytes=12 << 20),
        cost_estimate=pl.CostEstimate(flops=10_000_000, bytes_accessed=3 << 20, transcendentals=0),
    )(*arrays)


def window(pieces):
    stations, rows, times = pieces[0].shape
    shape = jax.ShapeDtypeStruct((stations // 2 * 3, 2, 2 * rows, times), BF16)
    return pl.pallas_call(
        window_kernel,
        in_specs=[VMEM] * len(pieces),
        out_specs=[VMEM, VMEM],
        out_shape=[shape, shape],
        compiler_params=pltpu.CompilerParams(vmem_limit_bytes=8 << 20),
        cost_estimate=pl.CostEstimate(flops=2_000_000, bytes_accessed=2 << 20, transcendentals=0),
    )(*pieces)


def products(flips, offsets, near, away, high_p, low_p):
    stations, _, height, times = away.shape
    columns = offsets.shape[1] * 2 * high_p.shape[2]
    return pl.pallas_call(
        functools.partial(product_kernel, flips),
        in_specs=[VMEM] * 5,
        out_specs=VMEM,
        out_shape=jax.ShapeDtypeStruct((stations * MAIN + 8, columns), F32),
        scratch_shapes=[pltpu.VMEM((stations, height, columns), F32)],
        compiler_params=pltpu.CompilerParams(vmem_limit_bytes=24 << 20),
        cost_estimate=pl.CostEstimate(
            flops=2 * 3 * stations * 2 * height * times * columns,
            bytes_accessed=4 << 20, transcendentals=0,
        ),
    )(offsets, near, away, high_p, low_p)


def close(parts, factor, count, azim):
    return pl.pallas_call(
        functools.partial(close_kernel, factor, count, azim),
        in_specs=[VMEM] * len(parts),
        out_specs=VMEM,
        out_shape=jax.ShapeDtypeStruct((1, count, LAGS * azim), F32),
        compiler_params=pltpu.CompilerParams(vmem_limit_bytes=4 << 20),
        cost_estimate=pl.CostEstimate(flops=1_000_000, bytes_accessed=1 << 18, transcendentals=0),
    )(*parts)


def shards(velocity, pressure, offsets):
    sta, rows, times = velocity.shape
    gx_n, az_n, ta_n = (lax.axis_size(name) for name in ("gx", "az", "ta"))
    assert az_n == 4 and ta_n == 4 and sta == az_n * ta_n
    azim = rows * az_n
    factor = 1.0 / math.sqrt(times * ta_n * azim)

    sibling = [(i, i ^ 1) for i in range(az_n)]
    across = [(i, i ^ 2) for i in range(az_n)]
    gx_az = [(g, a) for g in range(gx_n) for a in range(az_n)]
    flat = lambda g, a: (g % gx_n) * az_n + a
    upstream = [(g, (g - 1) % gx_n) for g in range(gx_n)]
    diagonal = [(flat(g, a), flat(g - 1, a ^ 2)) for g, a in gx_az]
    pairs = (
        [i ^ 1 if (i ^ 1) < ta_n else i for i in range(ta_n)],
        [min(max(((i + 1) ^ 1) - 1, 0), ta_n - 1) for i in range(ta_n)],
    )
    az_ta = [(a, t) for a in range(az_n) for t in range(ta_n)]
    in_time = [(a * ta_n + t, a * ta_n + pairs[a % 2][t]) for a, t in az_ta]
    in_time_across = [(a * ta_n + t, (a ^ 2) * ta_n + pairs[a % 2][t]) for a, t in az_ta]

    to_sibling = lambda x: lax.ppermute(x, "az", sibling)

    diag = lax.ppermute(pressure, ("gx", "az"), diagonal)
    far = lax.ppermute(pressure, "az", across)
    p_sib = to_sibling(pressure)
    v_sib = to_sibling(velocity)
    up = lax.ppermute(pressure, "gx", upstream)
    vel, v_for, ends_near, ends_away = fetch(velocity, v_sib)
    ends_near, ends_away = lax.optimization_barrier((ends_near, ends_away))
    h_near = lax.ppermute(ends_near, ("az", "ta"), in_time)
    v_far = lax.ppermute(v_for, "az", across)
    h_away = lax.ppermute(ends_away, ("az", "ta"), in_time_across)
    diag, h_away, h_near, up, far = lax.optimization_barrier((diag, h_away, h_near, up, far))
    both = jnp.stack([h_near, h_away])
    v_far, far = lax.optimization_barrier((v_far, far))
    up_sib = to_sibling(up)
    v_far_sib = to_sibling(v_far)
    diag_sib = to_sibling(diag)
    far_sib = to_sibling(far)
    both_sib = to_sibling(both)
    h_near_sib, h_away_sib = both_sib[0], both_sib[1]
    own = (vel, v_sib, h_near, h_near_sib)
    high_p, low_p = window([pressure, up, far, diag, p_sib, up_sib, far_sib, diag_sib])
    series = (v_far, v_far_sib, h_away, h_away_sib)

    offsets = offsets.reshape(1, -1)
    flips = (1, 3)
    give = products(flips, offsets, lag_rows(flips, False, *own), lag_rows(flips, True, *series), high_p, low_p)
    first = lax.ppermute(give, "ta", [(i, i ^ 1) for i in range(ta_n)])
    flips = (0, 2)
    keep = [
        products((flip,), offsets, lag_rows((flip,), False, *own), lag_rows((flip,), True, *series), high_p, low_p)
        for flip in (2, 0)
    ]
    second = lax.ppermute(keep[0] + first[MAIN:], "ta", [(i, i ^ 2) for i in range(ta_n)])
    return close([keep[1], first, second], factor, offsets.shape[1], azim)


def solution(mesh):
    return jax.shard_map(
        shards,
        mesh=mesh,
        in_specs=(P("gx", "az", "ta"), P("gx", "az", "ta"), P()),
        out_specs=P(("gx", "az", "ta"), None, None),
        check_vma=False,
    )
```

```python
import functools
import math

import jax
import jax.numpy as jnp
from jax import lax
from jax.experimental import pallas as pl
from jax.experimental.pallas import tpu as pltpu
from jax.sharding import PartitionSpec as P

MAXLAG = 16
LAGS = 2 * MAXLAG + 1
MAIN = 2 * MAXLAG
LANES = 128
BF16 = jnp.bfloat16
F32 = jnp.float32


def position():
    az, ta = lax.axis_index("az"), lax.axis_index("ta")
    return az, lax.rem(az, 2), lax.div(az, 2), ta


def split(x):
    high = x.astype(BF16)
    return high, (x - high.astype(F32)).astype(BF16)


def in_core_order(core, mine, other):
    first = jnp.where(core == 0, mine, other)
    second = jnp.where(core == 0, other, mine)
    return jnp.concatenate([first, second], axis=0)


def fetch_kernel(velocity, v_sib, out, part, ends_near, ends_away):
    half = part.shape[0]
    _, core, row_y, ta = position()
    right = lax.rem(ta + core, 2) == 0
    times = velocity.shape[2]
    for i in range(half):
        part[i] = velocity[(1 - row_y) * half + i]
    out[...] = velocity[...]
    lane = lax.broadcasted_iota(jnp.int32, ends_near.shape, 1) // MAXLAG
    for ends, first in ((ends_near, row_y * half), (ends_away, (1 - row_y) * half)):
        acc = jnp.zeros(ends_near.shape, F32)
        for j in range(half):
            def tile(lo):
                return in_core_order(core, velocity[first + j, :, lo : lo + LANES], v_sib[first + j, :, lo : lo + LANES])

            edge = jnp.where(right, pltpu.roll(tile(times - LANES), MAXLAG, 1), tile(0))
            edge = pltpu.roll(edge, MAXLAG * j, 1) if j else edge
            acc = jnp.where(lane == j, edge, acc)
        ends[...] = acc


def halo_tile(station, mine, other):
    _, core, _, ta = position()
    swap = lax.rem(ta + core, 2) == 0
    last = lax.axis_size("ta") - 1
    before = jnp.where(swap, other, mine) * jnp.where(ta == 0, 0.0, 1.0).astype(F32)
    after = jnp.where(swap, mine, other) * jnp.where(ta == last, 0.0, 1.0).astype(F32)
    start = lax.rem(LANES - MAXLAG * station, LANES)
    after = pltpu.roll(after, start, 1)
    before = pltpu.roll(before, lax.rem(start + LANES - MAXLAG, LANES), 1)
    lane = lax.broadcasted_iota(jnp.int32, after.shape, 1)
    return jnp.where(lane < LANES // 2, after, before)


def lag_kernel(flips, away, v_a, v_b, h_a, h_b, out):
    az, core, row_y, place = position()
    rows, times = v_a.shape[1:]
    mine = lax.axis_size("ta")
    width = times + LANES
    for i in range(out.shape[0]):
        station = i if flips is None else place ^ flips[i]
        in_chip = mine * core + station
        at_v = in_chip if away else mine * az + station
        series = in_core_order(core, v_a[at_v], v_b[at_v])
        edges = halo_tile(in_chip, h_a[...], h_b[...])
        series = jnp.concatenate([series, edges], axis=1)
        for b in range(2 * rows):
            line = jnp.broadcast_to(series[b : b + 1, :], (8, width))
            for half in range(MAIN // 16):
                parts = [
                    pltpu.roll(line, (8 * g - MAXLAG) % width, 1, stride=1, stride_axis=0)[:, :times]
                    for g in (2 * half, 2 * half + 1)
                ]
                high, low = split(jnp.concatenate(parts, axis=0))
                row = b * MAIN + 16 * half
                out[i, 0, row : row + 16, :] = high
                out[i, 1, row : row + 16, :] = low
        high, low = split(pltpu.roll(series, MAXLAG, 1)[:, :times])
        row = 2 * rows * MAIN
        out[i, 0, row : row + 2 * rows, :] = high
        out[i, 1, row : row + 2 * rows, :] = low


def window_kernel(o_own, u_own, o_far, u_far, o_sib, u_sib, o_far_sib, u_far_sib, high_p, low_p):
    _, core, row_y, _ = position()
    last_gx = lax.axis_index("gx") == lax.axis_size("gx") - 1
    half = o_own.shape[0] // 2
    keep_up = jnp.where(last_gx, 0.0, 1.0).astype(F32)
    keep_mid = jnp.where(last_gx & (row_y == 1), 0.0, 1.0).astype(F32)
    near = (o_own, u_own, o_sib, u_sib, row_y)
    away = (o_far, u_far, o_far_sib, u_far_sib, 1 - row_y)

    def one(w, carry):
        shift = row_y * half + w
        for o_a, u_a, o_b, u_b, at in (near, away):
            low_slot = in_core_order(core, o_a[shift], o_b[shift])
            middle = in_core_order(
                core,
                jnp.where(row_y == 0, o_a[half + w], u_a[w]),
                jnp.where(row_y == 0, o_b[half + w], u_b[w]),
            )
            high_slot = in_core_order(core, u_a[shift], u_b[shift])
            for slot, x in enumerate((low_slot, middle * keep_mid, high_slot * keep_up)):
                high, low = split(x)
                high_p[slot * half + w, at] = high
                low_p[slot * half + w, at] = low
        return carry

    lax.fori_loop(0, half, one, 0)


def product_kernel(flips, offsets, lags_near, lags_away, high_p, low_p, out, prod):
    _, core, row_y, place = position()
    half = high_p.shape[0] // 3
    rows, azim = high_p.shape[2] // 2, 2 * high_p.shape[2]
    count = offsets.shape[1]
    for i, flip in enumerate(flips):
        station = place ^ flip
        first = (half // 2) * core + station
        right = []
        for turned in (row_y, 1 - row_y):
            tiles = {0: [], 1: []}
            for k in range(count):
                w = first + offsets[0, k]
                for which, source in ((0, high_p), (1, low_p)):
                    tiles[which] += [source[w, turned], source[w, 1 - turned]]
            high = jnp.concatenate(tiles[0], axis=0)
            low = jnp.concatenate(tiles[1], axis=0)
            right += [high, low, high]
        right = jnp.concatenate(right, axis=1)
        left = []
        for lags, at in ((lags_near, i), (lags_away, i)):
            left += [lags[at, 0], lags[at, 0], lags[at, 1]]
        left = jnp.concatenate(left, axis=1)
        middle = rows * MAIN
        for part in (slice(0, middle), slice(middle, left.shape[0])):
            prod[i, part] = lax.dot_general(
                left[part], right, (((1,), (1,)), ((), ())), preferred_element_type=F32
            )
        sums = diagonals(prod.at[i], rows, azim, count)
        out[i * MAIN : (i + 1) * MAIN] = sums[:MAIN]
        end = sums[MAIN:]
        tail = end if i == 0 else jnp.where(lax.broadcasted_iota(jnp.int32, end.shape, 0) < i, tail, end)
    out[len(flips) * MAIN :] = tail


def diagonals(prod, rows, azim, count):
    lane = lax.broadcasted_iota(jnp.int32, (1, LANES), 1) % azim
    pieces = []
    for c in range(0, count * azim, LANES):
        inside = prod[:MAIN, c : c + LANES]
        beyond = jnp.zeros_like(inside)
        for b in range(1, 2 * rows):
            moved = pltpu.roll(prod[b * MAIN : (b + 1) * MAIN, c : c + LANES], LANES - b, 1)
            inside += jnp.where(lane < azim - b, moved, 0.0)
            beyond += jnp.where(lane < azim - b, 0.0, moved)
        extra = prod[2 * rows * MAIN : 2 * rows * (MAIN + 1), c : c + LANES]
        row = lax.broadcasted_iota(jnp.int32, extra.shape, 0)
        moved, by = extra, 1
        while by < 2 * rows:
            moved = jnp.where((row & by) != 0, pltpu.roll(moved, LANES - by, 1), moved)
            by *= 2
        ends = [
            jnp.broadcast_to(jnp.sum(jnp.where(keep, moved, 0.0), axis=0, keepdims=True), (8, LANES))
            for keep in (lane < azim - row, lane >= azim - row)
        ]
        inside = jnp.concatenate([inside, ends[0]], axis=0)
        beyond = jnp.concatenate([beyond, ends[1]], axis=0)
        pieces.append(inside + pltpu.roll(beyond, azim, 1))
    return jnp.concatenate(pieces, axis=1)


def close_kernel(factor, count, azim, *refs):
    mine, first, second, out = refs
    total = (mine[:MAIN] + first[:MAIN] + second[:MAIN]) * factor
    last = 2 * MAIN
    tail = (mine[MAIN : MAIN + 1] + first[last : last + 1] + second[MAIN + 1 : MAIN + 2]) * factor
    groups = LANES // azim
    lane = lax.broadcasted_iota(jnp.int32, (count, LANES), 1) // azim
    sub = lax.broadcasted_iota(jnp.int32, (count, LANES), 0)
    for tile in range(-(-LAGS // groups)):
        acc = jnp.zeros((count, LANES), F32)
        for j in range(groups):
            tau = tile * groups + j
            if tau >= LAGS:
                continue
            x = jnp.zeros((count, LANES), F32)
            for part in range(count // groups):
                source = total[tau : tau + 1] if tau < MAIN else tail
                line = source[:, part * LANES : (part + 1) * LANES]
                x = jnp.where(sub // groups == part, jnp.broadcast_to(line, (count, LANES)), x)
            moved = x
            for s in range(groups):
                by = ((j - s) * azim) % LANES
                shifted = pltpu.roll(x, by, 1) if by else x
                moved = jnp.where(sub % groups == s, shifted, moved)
            acc = jnp.where(lane == j, moved, acc)
        width = min(LANES, (LAGS - tile * groups) * azim)
        out[0, :, tile * LANES : tile * LANES + width] = acc[:, :width]


VMEM = pl.BlockSpec(memory_space=pltpu.VMEM)


def fetch(velocity, v_sib):
    stations, rows, times = velocity.shape
    shapes = [
        (stations, rows, times), (stations // 2, rows, times),
        (2 * rows, stations // 2 * MAXLAG), (2 * rows, stations // 2 * MAXLAG),
    ]
    return pl.pallas_call(
        fetch_kernel,
        in_specs=[VMEM, VMEM],
        out_specs=[VMEM] * len(shapes),
        out_shape=[jax.ShapeDtypeStruct(shape, F32) for shape in shapes],
        compiler_params=pltpu.CompilerParams(vmem_limit_bytes=2 << 20),
        cost_estimate=pl.CostEstimate(flops=0, bytes_accessed=1 << 19, transcendentals=0),
    )(velocity, v_sib)


def lag_rows(flips, away, *arrays):
    rows, times = arrays[0].shape[1:]
    stations = lax.axis_size("ta") if flips is None else len(flips)
    shape = (stations, 2, 2 * rows * (MAIN + 1), times)
    return pl.pallas_call(
        functools.partial(lag_kernel, flips, away),
        in_specs=[VMEM] * len(arrays),
        out_specs=VMEM,
        out_shape=jax.ShapeDtypeStruct(shape, BF16),
        compiler_params=pltpu.CompilerParams(vmem_limit_bytes=12 << 20),
        cost_estimate=pl.CostEstimate(flops=10_000_000, bytes_accessed=3 << 20, transcendentals=0),
    )(*arrays)


def window(pieces):
    stations, rows, times = pieces[0].shape
    shape = jax.ShapeDtypeStruct((stations // 2 * 3, 2, 2 * rows, times), BF16)
    return pl.pallas_call(
        window_kernel,
        in_specs=[VMEM] * len(pieces),
        out_specs=[VMEM, VMEM],
        out_shape=[shape, shape],
        compiler_params=pltpu.CompilerParams(vmem_limit_bytes=8 << 20),
        cost_estimate=pl.CostEstimate(flops=2_000_000, bytes_accessed=2 << 20, transcendentals=0),
    )(*pieces)


def products(flips, offsets, near, away, high_p, low_p):
    stations, _, height, times = away.shape
    columns = offsets.shape[1] * 2 * high_p.shape[2]
    return pl.pallas_call(
        functools.partial(product_kernel, flips),
        in_specs=[VMEM] * 5,
        out_specs=VMEM,
        out_shape=jax.ShapeDtypeStruct((stations * MAIN + 8, columns), F32),
        scratch_shapes=[pltpu.VMEM((stations, height, columns), F32)],
        compiler_params=pltpu.CompilerParams(vmem_limit_bytes=24 << 20),
        cost_estimate=pl.CostEstimate(
            flops=2 * 3 * stations * 2 * height * times * columns,
            bytes_accessed=4 << 20, transcendentals=0,
        ),
    )(offsets, near, away, high_p, low_p)


def close(parts, factor, count, azim):
    return pl.pallas_call(
        functools.partial(close_kernel, factor, count, azim),
        in_specs=[VMEM] * len(parts),
        out_specs=VMEM,
        out_shape=jax.ShapeDtypeStruct((1, count, LAGS * azim), F32),
        compiler_params=pltpu.CompilerParams(vmem_limit_bytes=4 << 20),
        cost_estimate=pl.CostEstimate(flops=1_000_000, bytes_accessed=1 << 18, transcendentals=0),
    )(*parts)


def shards(velocity, pressure, offsets):
    sta, rows, times = velocity.shape
    gx_n, az_n, ta_n = (lax.axis_size(name) for name in ("gx", "az", "ta"))
    assert az_n == 4 and ta_n == 4 and sta == az_n * ta_n
    azim = rows * az_n
    factor = 1.0 / math.sqrt(times * ta_n * azim)

    sibling = [(i, i ^ 1) for i in range(az_n)]
    across = [(i, i ^ 2) for i in range(az_n)]
    gx_az = [(g, a) for g in range(gx_n) for a in range(az_n)]
    flat = lambda g, a: (g % gx_n) * az_n + a
    upstream = [(g, (g - 1) % gx_n) for g in range(gx_n)]
    diagonal = [(flat(g, a), flat(g - 1, a ^ 2)) for g, a in gx_az]
    pairs = (
        [i ^ 1 if (i ^ 1) < ta_n else i for i in range(ta_n)],
        [min(max(((i + 1) ^ 1) - 1, 0), ta_n - 1) for i in range(ta_n)],
    )
    az_ta = [(a, t) for a in range(az_n) for t in range(ta_n)]
    in_time = [(a * ta_n + t, a * ta_n + pairs[a % 2][t]) for a, t in az_ta]
    in_time_across = [(a * ta_n + t, (a ^ 2) * ta_n + pairs[a % 2][t]) for a, t in az_ta]

    to_sibling = lambda x: lax.ppermute(x, "az", sibling)

    diag = lax.ppermute(pressure, ("gx", "az"), diagonal)
    far = lax.ppermute(pressure, "az", across)
    p_sib = to_sibling(pressure)
    v_sib = to_sibling(velocity)
    up = lax.ppermute(pressure, "gx", upstream)
    vel, v_for, ends_near, ends_away = fetch(velocity, v_sib)
    ends_near, ends_away = lax.optimization_barrier((ends_near, ends_away))
    h_near = lax.ppermute(ends_near, ("az", "ta"), in_time)
    v_far = lax.ppermute(v_for, "az", across)
    h_away = lax.ppermute(ends_away, ("az", "ta"), in_time_across)
    diag, h_away, h_near, up, far = lax.optimization_barrier((diag, h_away, h_near, up, far))
    both = jnp.stack([h_near, h_away])
    v_far, far = lax.optimization_barrier((v_far, far))
    up_sib = to_sibling(up)
    v_far_sib = to_sibling(v_far)
    diag_sib = to_sibling(diag)
    far_sib = to_sibling(far)
    both_sib = to_sibling(both)
    h_near_sib, h_away_sib = both_sib[0], both_sib[1]
    own = (vel, v_sib, h_near, h_near_sib)
    high_p, low_p = window([pressure, up, far, diag, p_sib, up_sib, far_sib, diag_sib])
    series = (v_far, v_far_sib, h_away, h_away_sib)

    offsets = offsets.reshape(1, -1)
    flips = (1, 3)
    give = products(flips, offsets, lag_rows(flips, False, *own), lag_rows(flips, True, *series), high_p, low_p)
    first = lax.ppermute(give, "ta", [(i, i ^ 1) for i in range(ta_n)])
    flips = (0, 2)
    keep = [
        products((flip,), offsets, lag_rows((flip,), False, *own), lag_rows((flip,), True, *series), high_p, low_p)
        for flip in (2, 0)
    ]
    second = lax.ppermute(keep[0] + first[MAIN:], "ta", [(i, i ^ 2) for i in range(ta_n)])
    return close([keep[1], first, second], factor, offsets.shape[1], azim)


def solution(mesh):
    return jax.shard_map(
        shards,
        mesh=mesh,
        in_specs=(P("gx", "az", "ta"), P("gx", "az", "ta"), P()),
        out_specs=P(("gx", "az", "ta"), None, None),
        check_vma=False,
    )
```
